32 devices in a mesh: blk: 4 (over y, x), wide: 8 (over z, core).
Axes of the slice: x: 2, y: 2, z: 4, core: 2. Of those that a mesh axis runs over, the one named last changes fastest.
Arguments:
- upstream: bfloat16 [3072, 7168], P('wide'), may hold values from -8 to 8
- gate_pre: bfloat16 [3072, 1024], P('wide', 'blk'), may hold values from -6 to 6
- up_pre: bfloat16 [3072, 1024], P('wide', 'blk'), may hold values from -8 to 8
- down_weight: bfloat16 [7168, 2, 1024], P(None, None, 'blk'), may hold values from -0.1875 to 0.1875
- block_expert: int32 [24], P('wide'), may hold values from 0 to 1
- row_token: int32 [3072], P('wide'), may hold values from 0 to 383, as said below
- gate_prob: float32 [3072], P('wide'), may hold values from 0.05 to 0.8
Outputs:
- down_grad: float32 [7168, 2, 1024], P('wide', None, 'blk')
- grad_rms: float32 [2], replicated
- prob_grad: float32 [3072], P('wide')
- gate_grad: bfloat16 [3072, 1024], P('wide', 'blk')
- up_grad: bfloat16 [3072, 1024], P('wide', 'blk')
The draws below stay inside these ranges and needn't reach their ends.
Inputs may be any that keep to these rules, and one draw needn't show every extreme that they name: Within each index of wide, row_token is a permutation of the 384 tokens held there: every token has exactly one routed row in the window.
All inputs are finite; a program needn't handle non-finite values.
Results may differ from the reference program's by a relative error of at most 0.0029.
Values sent between devices are 32-bit elements; how exact they have to be, the bound alone decides.
No kernel may reach another device: no remote copies, remote signals or barrier semaphores. Data moves between devices by JAX's collectives and lax.ppermute only.
A program may use at most 128 MiB of HBM per device.

```python
import math
import jax
import jax.numpy as jnp
from jax import lax

D = 7168
FFW = 1024
EXPERTS = 2
BLOCK = 128
ROWS = 384
ROWS_ALL = 3072
BLOCKS_ALL = 24


def draw_upstream(key, part):
    first_key, second_key = jax.random.split(key, 2)
    position = jnp.arange(D, dtype=jnp.float32) / (D - 1)
    trend = 1.0 + 2.0 * position
    base = jax.random.normal(first_key, (ROWS_ALL, D), jnp.float32)
    spread = jnp.exp(jax.random.uniform(second_key, (1, D), jnp.float32, 0.0, math.log(10.0)))
    return jnp.clip(0.04 * base * trend[None, :] * spread, -8.0, 8.0).astype(jnp.bfloat16)


def draw_up_pre(key, part):
    first_key, second_key = jax.random.split(key, 2)
    position = jnp.arange(FFW, dtype=jnp.float32) / (FFW - 1)
    trend = 1.0 + 2.0 * position
    base = jax.random.normal(first_key, (ROWS_ALL, FFW), jnp.float32)
    spread = jnp.exp(jax.random.uniform(second_key, (1, FFW), jnp.float32, math.log(0.3), math.log(3.0)))
    return jnp.clip(0.5 * base * trend[None, :] * spread, -8.0, 8.0).astype(jnp.bfloat16)


def draw_row_token(key, part):
    device_keys = jax.random.split(key, ROWS_ALL // ROWS)

    def one_device(device_key):
        return jax.random.permutation(device_key, ROWS)
    return jax.vmap(one_device)(device_keys).reshape(ROWS_ALL).astype(jnp.int32)


def plant(result, rng, low, high):
    spot = [jax.random.randint(jax.random.fold_in(rng, axis), (), 0, length) for axis, length in enumerate(result.shape)]
    widest = result.shape.index(max(result.shape))
    next_to = spot[:widest] + [(spot[widest] + 1) % result.shape[widest]] + spot[widest + 1:]
    return result.at[tuple(spot)].set(low).at[tuple(next_to)].set(high)


def block_scale(own_key, extent, cuts, least, top_value):
    def one(dim, shards_of):
        steps = jax.random.uniform(jax.random.fold_in(jax.random.fold_in(own_key, 6), dim), (shards_of,), jnp.float32, least / len(cuts), top_value / len(cuts))
        return jnp.repeat(jnp.exp(steps), extent[dim] // shards_of).reshape((-1,) + (1,) * (len(extent) - dim - 1))

    level = one(*cuts[0])
    for cut in cuts[1:]:
        level = level * one(*cut)
    return level


def bell_draw(key, extent, scale, bound, cuts=(), kind=jnp.bfloat16):
    drawn = jax.random.normal(key, extent, jnp.float32) * scale
    if len(cuts) > 0:
        drawn = block_scale(key, extent, cuts, -0.22, 0.18) * drawn
    return jnp.clip(drawn, min=-bound, max=bound).astype(kind)


def setup_inputs(seed: int = 0) -> dict:
    key_of = jax.random.split(jax.random.key(seed), 8)
    upstream = draw_upstream(jax.random.fold_in(key_of[7], 71), 0)
    gate_pre = bell_draw(key_of[1], (ROWS_ALL, FFW), 1.0, 6.0, ((0, 8), (1, 4)))
    up_pre = draw_up_pre(jax.random.fold_in(key_of[7], 71), 0)
    down_weight = bell_draw(key_of[3], (D, EXPERTS, FFW), FFW ** -0.5, 0.1875, ((2, 4),))
    block_expert = plant(jax.random.randint(key_of[4], (BLOCKS_ALL,), 0, EXPERTS), jax.random.fold_in(key_of[4], 1), 0, EXPERTS - 1).astype(jnp.int32)
    row_token = draw_row_token(jax.random.fold_in(key_of[7], 71), 0)
    gate_prob = jnp.clip(0.05 + 0.75 * jax.random.uniform(key_of[6], (ROWS_ALL,), jnp.float32) ** block_scale(key_of[6], (ROWS_ALL,), ((0, 8),), -0.2, 0.2), 0.05, 0.8)
    return dict(upstream=upstream, gate_pre=gate_pre, up_pre=up_pre, down_weight=down_weight, block_expert=block_expert, row_token=row_token, gate_prob=gate_prob)


def reference(upstream, gate_pre, up_pre, down_weight, block_expert, row_token, gate_prob):
    owner = jnp.arange(ROWS_ALL, dtype=jnp.int32) // ROWS
    token_index = (owner * ROWS + row_token.astype(jnp.int32)).astype(jnp.int32)
    routed = upstream[token_index]
    gate_value = gate_pre.astype(jnp.float32)
    up_value = up_pre.astype(jnp.float32)
    sigmoid_gate = jax.nn.sigmoid(gate_value)
    active = gate_value * sigmoid_gate
    hidden = active * up_value
    weighted = (hidden * gate_prob[:, None]).astype(jnp.bfloat16)
    routed_blocks = routed.reshape(BLOCKS_ALL, BLOCK, D)
    weighted_blocks = weighted.reshape(BLOCKS_ALL, BLOCK, FFW)

    def project(block_item):
        rows_block, expert_id = block_item
        weights = lax.dynamic_index_in_dim(down_weight, expert_id, 1, keepdims=False)
        return jnp.dot(rows_block, weights, preferred_element_type=jnp.float32)
    projected = lax.map(project, (routed_blocks, block_expert)).reshape(ROWS_ALL, FFW)
    scaled = gate_prob[:, None] * projected
    up_grad = (scaled * active).astype(jnp.bfloat16)
    gate_grad = (scaled * up_value * sigmoid_gate * (1.0 + gate_value * (1.0 - sigmoid_gate))).astype(jnp.bfloat16)
    prob_grad = lax.optimization_barrier(jnp.sum(hidden * projected, axis=1))

    def accumulate(running, block_item):
        rows_block, weighted_block, expert_id = block_item
        product = jnp.dot(rows_block.T, weighted_block, preferred_element_type=jnp.float32)
        current = lax.dynamic_index_in_dim(running, expert_id, 1, keepdims=True)
        return (lax.dynamic_update_index_in_dim(running, current + product[:, None, :], expert_id, 1), None)
    down_grad, _ = lax.scan(accumulate, jnp.zeros((D, EXPERTS, FFW), jnp.float32), (routed_blocks, weighted_blocks, block_expert))
    grad_rms = jnp.sqrt(lax.optimization_barrier(jnp.mean(down_grad * down_grad, axis=(0, 2))))
    return (down_grad, grad_rms, prob_grad, gate_grad, up_grad)
```

```python
import jax
import jax.numpy as jnp
from jax import lax
from jax.experimental import pallas as pl
from jax.experimental.pallas import tpu as pltpu
from jax.sharding import PartitionSpec as P

D = 7168
FFW = 1024
EXPERTS = 2
BLOCK = 128
Z_ORDER = (1, 3, 2)


def sums_body(upstream, gate_pre, up_pre, down_weight, block_expert, row_token, gate_prob):
    routed = upstream[row_token]
    row_count = routed.shape[0]
    block_count = row_count // BLOCK
    width = routed.shape[1]
    hidden_share = gate_pre.shape[1]
    gate_value = gate_pre.astype(jnp.float32)
    up_value = up_pre.astype(jnp.float32)
    sigmoid_gate = jax.nn.sigmoid(gate_value)
    active = gate_value * sigmoid_gate
    hidden = active * up_value
    weighted = (hidden * gate_prob[:, None]).astype(jnp.bfloat16)
    routed_blocks = routed.reshape(block_count, BLOCK, width)
    weighted_blocks = weighted.reshape(block_count, BLOCK, hidden_share)

    def project(block_item):
        rows_block, expert_id = block_item
        weights = lax.dynamic_index_in_dim(down_weight, expert_id, 1, keepdims=False)
        return jnp.dot(rows_block, weights, preferred_element_type=jnp.float32)

    projected = lax.map(project, (routed_blocks, block_expert)).reshape(row_count, hidden_share)
    scaled = gate_prob[:, None] * projected
    up_grad = (scaled * active).astype(jnp.bfloat16)
    gate_grad = (
        scaled * up_value * sigmoid_gate * (1.0 + gate_value * (1.0 - sigmoid_gate))
    ).astype(jnp.bfloat16)
    partial_value = jnp.sum(hidden * projected, axis=1)
    prob_grad = lax.psum(partial_value, "blk")
    row_share = width // lax.axis_size("wide")

    def select_columns(amount):
        return routed.reshape(block_count, BLOCK, amount)

    def block_product(columns, block_index):
        column_block = lax.dynamic_index_in_dim(columns, block_index, 0, keepdims=False)
        weighted_block = lax.dynamic_index_in_dim(weighted_blocks, block_index, 0, keepdims=False)
        return jnp.dot(column_block.T, weighted_block, preferred_element_type=jnp.float32)

    pieces = []
    for expert in range(EXPERTS):

        def one_expert(first, amount, expert=expert):
            columns = select_columns(amount)

            def add_block(block_index, running):
                expert_id = lax.dynamic_index_in_dim(block_expert, block_index, 0, keepdims=False)

                def with_block(running_sum):
                    return running_sum + block_product(columns, block_index)

                def without_block(running_sum):
                    return running_sum

                return lax.cond(expert_id == expert, with_block, without_block, running)

            start_value = jnp.zeros((amount, hidden_share), jnp.float32)
            return lax.fori_loop(0, block_count, add_block, start_value)

        pieces.append(
            lax.psum_scatter(
                one_expert(jnp.int32(0), lax.axis_size("wide") * row_share),
                "wide",
                scatter_dimension=0,
                tiled=True,
            )
        )
    down_grad = jnp.stack(pieces, axis=1)
    squares = jnp.sum(down_grad * down_grad, axis=(0, 2))
    total_sum = lax.psum(squares, ("blk", "wide"))
    grad_rms = jnp.sqrt(total_sum / float(D * FFW))
    return (down_grad, grad_rms, prob_grad, gate_grad, up_grad)


def add_products(parts, spots, right, total):
    depth = right.shape[0]
    share = parts[0].shape[-1]

    def kernel(*refs):
        part_refs, (right_ref, total_ref, out_ref, left) = refs[: len(parts)], refs[len(parts) :]
        for part_ref, spot in zip(part_refs, spots):
            if len(part_ref.shape) == 2:
                left[spot : spot + part_ref.shape[0], :] = part_ref[...].astype(jnp.bfloat16)
            else:
                for one in range(part_ref.shape[0]):
                    first = spot + one * (depth // part_ref.shape[0])
                    left[first : first + part_ref.shape[1], :] = part_ref[one].astype(jnp.bfloat16)
        weights = right_ref[...].astype(jnp.bfloat16)
        for first in range(0, share, 128):
            out_ref[first : first + 128, :] = total_ref[first : first + 128, :] + lax.dot_general(
                left[:, first : first + 128],
                weights,
                (((0,), (0,)), ((), ())),
                preferred_element_type=jnp.float32,
            )

    return pl.pallas_call(
        kernel,
        out_shape=jax.ShapeDtypeStruct(total.shape, jnp.float32),
        in_specs=[pl.BlockSpec(memory_space=pltpu.VMEM)] * (len(parts) + 2),
        out_specs=pl.BlockSpec(memory_space=pltpu.VMEM),
        scratch_shapes=[pltpu.VMEM((depth, share), jnp.bfloat16)],
        compiler_params=pltpu.CompilerParams(vmem_limit_bytes=24 * 1024 * 1024),
        cost_estimate=pl.CostEstimate(
            flops=2 * depth * share * right.shape[1],
            bytes_accessed=4 * depth * (share + right.shape[1]) + 8 * share * right.shape[1],
            transcendentals=0,
        ),
    )(*parts, right, total)


def factors_body(upstream, gate_pre, up_pre, down_weight, block_expert, row_token, gate_prob):
    rows, width = upstream.shape
    hidden_share = gate_pre.shape[1]
    columns = lax.axis_size("blk")
    wide = lax.axis_size("wide")
    chips = wide // 2
    quarter = rows // columns
    share = width // wide
    blk_index = lax.axis_index("blk")
    wide_index = lax.axis_index("wide")
    chip = wide_index // 2
    core = wide_index % 2

    def moved(value, target):
        pairs = []
        for b in range(columns):
            for z in range(chips):
                for c in range(2):
                    to = target(b, z, c)
                    if to is not None:
                        pairs.append((b * wide + z * 2 + c, to[0] * wide + to[1] * 2 + to[2]))
        return lax.ppermute(value, ("blk", "wide"), pairs)

    def along_x(value):
        return moved(value, lambda b, z, c: (b ^ 1, z, c))

    def along_y(value):
        return moved(value, lambda b, z, c: (b ^ 2, z, c))

    def across(value):
        return moved(value, lambda b, z, c: (b, z, 1 - c))

    def step_up(value):
        return moved(value, lambda b, z, c: (b, z + 1, c) if z + 1 < chips else None)

    def step_down(value):
        return moved(value, lambda b, z, c: (b, z - 1, c) if z > 0 else None)

    pieces = {}
    previous = []
    for offset in Z_ORDER:
        pair = []
        for flip in range(2):
            first_column = share * (2 * ((chip + offset) % chips) + (core ^ flip))
            piece = lax.dynamic_slice(upstream, (quarter * blk_index, first_column), (quarter, share))
            piece = piece.astype(jnp.float32)
            if len(previous) >= 2:
                piece, _ = lax.optimization_barrier((piece, previous[-2]))
            got = moved(
                piece,
                lambda b, z, c, offset=offset, flip=flip: (b, (z + offset) % chips, c ^ flip),
            )
            previous.append(got)
            pair.append(got)
        pieces[offset] = jnp.stack(pair)

    gathered = {}
    for offset in Z_ORDER:
        own = pieces[offset]
        from_x = along_x(own)
        from_y = along_y(own)
        half = quarter // 2
        first = along_y(from_x[:, :half])
        second = along_x(from_y[:, half:])
        gathered[offset] = (own, from_x, from_y, first, second)

    gate_value = gate_pre.astype(jnp.float32)
    up_value = up_pre.astype(jnp.float32)
    sigmoid_gate = jax.nn.sigmoid(gate_value)
    active = gate_value * sigmoid_gate
    hidden = active * up_value
    weighted = (hidden * gate_prob[:, None]).astype(jnp.bfloat16)
    expert_of_row = jnp.repeat(block_expert, BLOCK)

    place = lax.iota(jnp.int32, rows)
    token = quarter * (blk_index ^ (place // quarter)) + place % quarter
    choose = token[:, None] == row_token[None, :]
    weighted_tokens = jnp.dot(
        choose.astype(jnp.bfloat16), weighted, preferred_element_type=jnp.float32
    )
    expert_of_token = jnp.sum(jnp.where(choose, expert_of_row[None, :], 0), axis=1)
    lines = -(-rows // hidden_share)
    marks = jnp.zeros((8 * hidden_share,), jnp.float32).at[:rows].set(expert_of_token.astype(jnp.float32))
    factor = jnp.concatenate([weighted_tokens, marks.reshape(8, hidden_share)], axis=0)

    def split_factor(value):
        marked = value[rows : rows + lines].reshape(lines * hidden_share)[:rows]
        weight = value[:rows]
        sides = [jnp.where((marked == expert)[:, None], weight, 0.0) for expert in range(EXPERTS)]
        return jnp.concatenate(sides, axis=1)

    factor, _ = lax.optimization_barrier((factor, previous[-2]))
    ups, downs = [], []
    up_value_now, down_value_now = factor, factor
    for _ in range(chips - 1):
        up_value_now = step_up(up_value_now)
        down_value_now = step_down(down_value_now)
        ups.append(up_value_now)
        downs.append(down_value_now)

    def own_columns(of_core):
        first_column = share * (2 * chip + of_core)
        parts = [
            lax.dynamic_slice(upstream, (quarter * (blk_index ^ q), first_column), (quarter, share))
            for q in range(columns)
        ]
        return jnp.concatenate(parts, axis=0).astype(jnp.float32)

    own_tokens = own_columns(core)
    other_tokens = across(own_columns(1 - core))
    other_factor = across(factor)

    total = add_products(
        (own_tokens, other_tokens),
        (0, rows),
        jnp.concatenate([split_factor(factor), split_factor(other_factor)], axis=0),
        jnp.zeros((share, EXPERTS * hidden_share), jnp.float32),
    )
    spots = (0, quarter, 2 * quarter, 3 * quarter, 3 * quarter + quarter // 2)
    for offset in Z_ORDER:
        from_below = ups[offset - 1]
        from_above = downs[chips - offset - 1]
        here = from_below + from_above
        there = across(here)
        right = jnp.concatenate([split_factor(here), split_factor(there)], axis=0)
        total = add_products(gathered[offset], spots, right, total)

    down_grad = total.reshape(share, EXPERTS, hidden_share)
    squares = jnp.sum(down_grad * down_grad, axis=(0, 2))
    devices = columns * wide
    padded = jnp.zeros((1, 128), jnp.float32).at[0, :EXPERTS].set(squares)
    spread = lax.all_to_all(
        jnp.broadcast_to(padded, (devices, 128)), ("blk", "wide"), 0, 0, tiled=True
    )
    total_sum = jnp.sum(spread, axis=0)[:EXPERTS]
    grad_rms = jnp.sqrt(total_sum / float(D * FFW))

    both = [
        jnp.dot(upstream, down_weight[:, expert, :], preferred_element_type=jnp.float32)
        for expert in range(EXPERTS)
    ]
    natural = row_token[:, None] == lax.iota(jnp.int32, rows)[None, :]
    pick = natural.astype(jnp.float32)
    rows_of = [jnp.dot(pick, one, precision=lax.Precision.HIGHEST) for one in both]
    projected = jnp.where((expert_of_row == 0)[:, None], rows_of[0], rows_of[1])
    scaled = gate_prob[:, None] * projected
    up_grad = (scaled * active).astype(jnp.bfloat16)
    gate_grad = (
        scaled * up_value * sigmoid_gate * (1.0 + gate_value * (1.0 - sigmoid_gate))
    ).astype(jnp.bfloat16)
    partial_value = jnp.sum(hidden * projected, axis=1)
    partial_value = partial_value + along_x(partial_value)
    prob_grad = partial_value + along_y(partial_value)
    return (down_grad, grad_rms, prob_grad, gate_grad, up_grad)


def solution(mesh):
    columns, wide = mesh.shape["blk"], mesh.shape["wide"]

    def body(upstream, gate_pre, up_pre, down_weight, block_expert, row_token, gate_prob):
        rows, width = upstream.shape
        hidden_share = gate_pre.shape[1]
        factors = wide * rows * (hidden_share + width // wide)
        sums = EXPERTS * width * hidden_share
        plan = factors_body if columns == 4 and wide == 8 and factors < sums else sums_body
        return plan(upstream, gate_pre, up_pre, down_weight, block_expert, row_token, gate_prob)

    in_specs = (
        P("wide", None),
        P("wide", "blk"),
        P("wide", "blk"),
        P(None, None, "blk"),
        P("wide"),
        P("wide"),
        P("wide"),
    )
    out_specs = (P("wide", None, "blk"), P(), P("wide"), P("wide", "blk"), P("wide", "blk"))
    return jax.shard_map(body, mesh=mesh, in_specs=in_specs, out_specs=out_specs, check_vma=False)
```

```python
import jax
import jax.numpy as jnp
from jax import lax
from jax.experimental import pallas as pl
from jax.experimental.pallas import tpu as pltpu
from jax.sharding import PartitionSpec as P

D = 7168
FFW = 1024
EXPERTS = 2
BLOCK = 128
VMEM = 56 * 1024 * 1024
EARLY = 20_000_000_000


def add_products(parts, pieces, here, there, total, rows, devices=0):
    depth = 2 * rows
    share = parts[0].shape[-1]
    hidden_share = here.shape[1]

    def kernel(*refs):
        part_refs, (here_ref, there_ref, total_ref, out_ref) = refs[: len(parts)], refs[len(parts) : len(parts) + 4]
        left, right = refs[-2:]
        for part, first, amount, spot in pieces:
            left[spot : spot + amount, :] = part_refs[part][first : first + amount, :].astype(jnp.bfloat16)
        for side, factor_ref in enumerate((here_ref, there_ref)):
            marks = factor_ref[rows:, :].T
            for first in range(0, rows, hidden_share):
                amount = min(hidden_share, rows - first)
                line = first // hidden_share
                mark = marks[:amount, line : line + 1]
                weight = factor_ref[first : first + amount, :]
                spot = side * rows + first
                for expert in range(EXPERTS):
                    right[spot : spot + amount, expert * hidden_share : (expert + 1) * hidden_share] = jnp.where(
                        mark == float(expert), weight, 0.0
                    ).astype(jnp.bfloat16)
        weights = right[...]
        squares = jnp.zeros((1, EXPERTS * hidden_share), jnp.float32)
        for first in range(0, share, 128):
            block = total_ref[first : first + 128, :] + lax.dot_general(
                left[:, first : first + 128],
                weights,
                (((0,), (0,)), ((), ())),
                preferred_element_type=jnp.float32,
            )
            out_ref[first : first + 128, :] = block
            if devices:
                squares = squares + jnp.sum(block * block, axis=0, keepdims=True)
        if devices:
            lane = lax.broadcasted_iota(jnp.int32, (devices, 128), 1)
            sums = jnp.zeros((devices, 128), jnp.float32)
            for expert in range(EXPERTS):
                own = squares[:, expert * hidden_share : (expert + 1) * hidden_share]
                sums = jnp.where(lane == expert, jnp.sum(own, axis=1, keepdims=True), sums)
            refs[-3][...] = sums

    out_shape = [jax.ShapeDtypeStruct(total.shape, jnp.float32)]
    if devices:
        out_shape.append(jax.ShapeDtypeStruct((devices, 128), jnp.float32))
    results = pl.pallas_call(
        kernel,
        out_shape=out_shape,
        in_specs=[pl.BlockSpec(memory_space=pltpu.VMEM)] * (len(parts) + 3),
        out_specs=[pl.BlockSpec(memory_space=pltpu.VMEM)] * len(out_shape),
        scratch_shapes=[
            pltpu.VMEM((depth, share), jnp.bfloat16),
            pltpu.VMEM((depth, EXPERTS * hidden_share), jnp.bfloat16),
        ],
        compiler_params=pltpu.CompilerParams(vmem_limit_bytes=16 * 1024 * 1024),
        cost_estimate=pl.CostEstimate(
            flops=2 * depth * share * EXPERTS * hidden_share,
            bytes_accessed=4 * depth * (share + hidden_share) + 8 * share * EXPERTS * hidden_share,
            transcendentals=0,
        ),
    )(*parts, here, there, total)
    return results if devices else results[0]


def stack_rows(lists, flops=0):
    arrays = []
    for pieces in lists:
        for array, _, _ in pieces:
            if not any(array is one for one in arrays):
                arrays.append(array)
    places = [
        [([array is one for one in arrays].index(True), first, amount) for array, first, amount in pieces]
        for pieces in lists
    ]
    share = arrays[0].shape[1]
    heights = [sum(amount for _, _, amount in pieces) for pieces in lists]

    def kernel(*refs):
        for out_ref, pieces in zip(refs[len(arrays) :], places):
            spot = 0
            for index, first, amount in pieces:
                out_ref[spot : spot + amount, :] = refs[index][first : first + amount, :]
                spot += amount

    return pl.pallas_call(
        kernel,
        out_shape=[jax.ShapeDtypeStruct((height, share), jnp.float32) for height in heights],
        in_specs=[pl.BlockSpec(memory_space=pltpu.VMEM)] * len(arrays),
        out_specs=[pl.BlockSpec(memory_space=pltpu.VMEM)] * len(lists),
        compiler_params=pltpu.CompilerParams(vmem_limit_bytes=12 * 1024 * 1024),
        cost_estimate=pl.CostEstimate(flops=flops, bytes_accessed=8 * sum(heights) * share, transcendentals=0),
    )(*arrays)


def project(upstream, weights):
    rows, width = upstream.shape
    hidden_share = weights.shape[2]
    steps = 7 if width % (7 * 128) == 0 else 1
    block = width // steps

    def kernel(upstream_ref, weights_ref, out_ref):
        @pl.when(pl.program_id(0) == 0)
        def _():
            out_ref[...] = jnp.zeros_like(out_ref)

        for expert in range(EXPERTS):
            out_ref[expert] += jnp.dot(
                upstream_ref[...], weights_ref[expert], preferred_element_type=jnp.float32
            )

    return pl.pallas_call(
        kernel,
        out_shape=jax.ShapeDtypeStruct((EXPERTS, rows, hidden_share), jnp.float32),
        grid=(steps,),
        in_specs=[
            pl.BlockSpec((rows, block), lambda i: (0, i)),
            pl.BlockSpec((EXPERTS, block, hidden_share), lambda i: (0, i, 0)),
        ],
        out_specs=pl.BlockSpec((EXPERTS, rows, hidden_share), lambda i: (0, 0, 0)),
        compiler_params=pltpu.CompilerParams(vmem_limit_bytes=VMEM),
        cost_estimate=pl.CostEstimate(
            flops=2 * rows * width * EXPERTS * hidden_share,
            bytes_accessed=2 * width * (rows + EXPERTS * hidden_share),
            transcendentals=0,
        ),
    )(upstream, weights)


def expert_line(expert_ref, rows):
    block = lax.broadcasted_iota(jnp.int32, (1, rows), 1) // BLOCK
    line = jnp.zeros((1, rows), jnp.float32)
    for index in range(rows // BLOCK):
        line = jnp.where(block == index, expert_ref[index].astype(jnp.float32), line)
    return line


def column_of(line):
    return jnp.broadcast_to(line, (8, line.shape[1])).T[:, :1]


def factor_of_tokens(gate_pre, up_pre, gate_prob, row_token, block_expert, blk_index, columns):
    rows, hidden_share = gate_pre.shape
    quarter = rows // columns

    def kernel(expert_ref, index_ref, gate_ref, up_ref, prob_ref, token_ref, out_ref):
        gate_value = gate_ref[...].astype(jnp.float32)
        hidden = gate_value * jax.nn.sigmoid(gate_value) * up_ref[...].astype(jnp.float32)
        weighted = (hidden * column_of(prob_ref[...].reshape(1, rows))).astype(jnp.bfloat16)
        place = lax.broadcasted_iota(jnp.int32, (rows, rows), 0)
        part = place // quarter
        token = (index_ref[0] ^ part) * quarter + (place - part * quarter)
        choose = jnp.where(token == token_ref[...].reshape(1, rows), 1.0, 0.0).astype(jnp.bfloat16)
        out_ref[:rows, :] = jnp.dot(choose, weighted, preferred_element_type=jnp.float32)
        experts = jnp.broadcast_to(expert_line(expert_ref, rows), (8, rows)).astype(jnp.bfloat16)
        marks = lax.dot_general(
            experts, choose, (((1,), (1,)), ((), ())), preferred_element_type=jnp.float32
        )
        out_ref[rows:, :] = jnp.zeros((8, hidden_share), jnp.float32)
        for first in range(0, rows, hidden_share):
            amount = min(hidden_share, rows - first)
            line = rows + first // hidden_share
            out_ref[line : line + 1, :amount] = marks[:1, first : first + amount]

    smem, vmem = pl.BlockSpec(memory_space=pltpu.SMEM), pl.BlockSpec(memory_space=pltpu.VMEM)
    return pl.pallas_call(
        kernel,
        out_shape=jax.ShapeDtypeStruct((rows + 8, hidden_share), jnp.float32),
        in_specs=[smem] * 2 + [vmem] * 4,
        out_specs=vmem,
        compiler_params=pltpu.CompilerParams(vmem_limit_bytes=VMEM),
        cost_estimate=pl.CostEstimate(flops=2 * rows * rows * hidden_share, bytes_accessed=12 * rows * hidden_share, transcendentals=0),
    )(block_expert, blk_index.reshape(1), gate_pre, up_pre, gate_prob, row_token)


def row_gradients(both, gate_pre, up_pre, gate_prob, row_token, block_expert):
    rows, hidden_share = gate_pre.shape

    def kernel(expert_ref, both_ref, gate_ref, up_ref, prob_ref, token_ref, up_grad_ref, gate_grad_ref, part_ref):
        place = lax.broadcasted_iota(jnp.int32, (rows, rows), 0)
        mine = place == token_ref[...].reshape(1, rows)
        expert_of_token = jnp.sum(jnp.where(mine, expert_line(expert_ref, rows), 0.0), axis=1, keepdims=True)
        of_token = both_ref[0]
        for expert in range(1, EXPERTS):
            of_token = jnp.where(expert_of_token == float(expert), both_ref[expert], of_token)
        choose = jnp.where(mine, 1.0, 0.0).astype(jnp.bfloat16)
        projected = jnp.zeros((rows, hidden_share), jnp.float32)
        rest = of_token
        for _ in range(3):
            top = rest.astype(jnp.bfloat16)
            projected = projected + lax.dot_general(
                choose, top, (((0,), (0,)), ((), ())), preferred_element_type=jnp.float32
            )
            rest = rest - top.astype(jnp.float32)
        gate_value = gate_ref[...].astype(jnp.float32)
        up_value = up_ref[...].astype(jnp.float32)
        sigmoid_gate = jax.nn.sigmoid(gate_value)
        active = gate_value * sigmoid_gate
        scaled = column_of(prob_ref[...].reshape(1, rows)) * projected
        up_grad_ref[...] = (scaled * active).astype(jnp.bfloat16)
        gate_grad_ref[...] = (
            scaled * up_value * sigmoid_gate * (1.0 + gate_value * (1.0 - sigmoid_gate))
        ).astype(jnp.bfloat16)
        part = jnp.sum(active * up_value * projected, axis=1, keepdims=True)
        part_ref[...] = jnp.broadcast_to(part, (rows, 128)).T[:8, :]

    smem, vmem = pl.BlockSpec(memory_space=pltpu.SMEM), pl.BlockSpec(memory_space=pltpu.VMEM)
    return pl.pallas_call(
        kernel,
        out_shape=[
            jax.ShapeDtypeStruct((rows, hidden_share), jnp.bfloat16),
            jax.ShapeDtypeStruct((rows, hidden_share), jnp.bfloat16),
            jax.ShapeDtypeStruct((8, rows), jnp.float32),
        ],
        in_specs=[smem] + [vmem] * 5,
        out_specs=[vmem] * 3,
        compiler_params=pltpu.CompilerParams(vmem_limit_bytes=VMEM),
        cost_estimate=pl.CostEstimate(flops=6 * rows * rows * hidden_share, bytes_accessed=20 * rows * hidden_share, transcendentals=0),
    )(block_expert, both, gate_pre, up_pre, gate_prob, row_token)


def together(*values):
    return lax.optimization_barrier(values)


def factors_body(upstream, gate_pre, up_pre, down_weight, block_expert, row_token, gate_prob):
    rows, width = upstream.shape
    hidden_share = gate_pre.shape[1]
    columns = lax.axis_size("blk")
    wide = lax.axis_size("wide")
    chips = wide // 2
    quarter = rows // columns
    half = quarter // 2
    share = width // wide
    blk_index = lax.axis_index("blk")
    wide_index = lax.axis_index("wide")
    chip = wide_index // 2
    core = wide_index % 2

    def moved(value, target):
        pairs = []
        for b in range(columns):
            for z in range(chips):
                for c in range(2):
                    to = target(b, z, c)
                    pairs.append((b * wide + z * 2 + c, to[0] * wide + to[1] * 2 + to[2]))
        return lax.ppermute(value, ("blk", "wide"), pairs)

    def along_x(value):
        return moved(value, lambda b, z, c: (b ^ 1, z, c))

    def along_y(value):
        return moved(value, lambda b, z, c: (b ^ 2, z, c))

    def across(value):
        return moved(value, lambda b, z, c: (b, z, 1 - c))

    def outer_swap(value):
        return moved(value, lambda b, z, c: (b, z ^ 1, c))

    def middle_swap(value):
        return moved(value, lambda b, z, c: (b, 3 - z, c) if 0 < z < 3 else (b, z, 1 - c))

    def piece_for(key, index):
        offset, flip = key
        first_column = share * (2 * (chip ^ offset) + (core ^ flip))
        piece = lax.dynamic_slice(upstream, (quarter * index, first_column), (quarter, share))
        return piece.astype(jnp.float32)

    def sent(key, piece):
        offset, flip = key
        return moved(piece, lambda b, z, c: (b, z ^ offset, c ^ flip))

    near_0 = sent((1, 0), piece_for((1, 0), blk_index))
    skip_0 = sent((2, 0), piece_for((2, 0), blk_index))
    (spread,) = stack_rows([[(near_0, 0, quarter), (skip_0, 0, quarter)]], EARLY)

    factor = factor_of_tokens(gate_pre, up_pre, gate_prob, row_token, block_expert, blk_index, columns)

    def own_columns(of_core, index):
        first_column = share * (2 * chip + of_core)
        parts = [
            lax.dynamic_slice(upstream, (quarter * (index ^ q), first_column), (quarter, share))
            for q in range(columns)
        ]
        return jnp.concatenate(parts, axis=0).astype(jnp.float32)

    factor_near = outer_swap(factor)
    mid_own = middle_swap(factor)
    down_weight, _ = together(down_weight, factor)
    spread, index = together(spread, blk_index)
    weights = jnp.transpose(down_weight, (1, 0, 2))
    pieces = [piece_for(key, index) for key in ((1, 1), (2, 1), (3, 0), (3, 1))]
    own_tokens, other_tokens = own_columns(core, index), own_columns(1 - core, index)
    other_factor = across(factor)

    spread, factor_near, mid_own, other_factor, weights, pieces, other_tokens = together(
        spread, factor_near, mid_own, other_factor, weights, pieces, other_tokens
    )
    piece_11, piece_21, piece_30, piece_31 = pieces
    near_1 = sent((1, 1), piece_11)
    skip_1 = sent((2, 1), piece_21)
    x_0, y_0 = along_x(spread), along_y(spread)
    (pair,) = stack_rows([[(near_1, 0, quarter), (skip_1, 0, quarter)]], EARLY)
    both = project(upstream, weights)
    other_tokens = across(other_tokens)

    (
        pair, x_0, y_0, both, factor_near, mid_own, other_tokens, piece_30, piece_31, gate_pre
    ) = together(
        pair, x_0, y_0, both, factor_near, mid_own, other_tokens, piece_30, piece_31, gate_pre
    )
    far_0 = sent((3, 0), piece_30)
    (far_0,) = stack_rows([[(far_0, 0, quarter)]], EARLY)
    mid_near = middle_swap(factor_near)
    to_x, to_y = stack_rows(
        [
            [(pair, 0, 2 * quarter), (y_0, quarter, quarter)],
            [(pair, 0, 2 * quarter), (x_0, 0, quarter)],
        ]
    )
    x_1, y_1 = along_x(to_x), along_y(to_y)
    out_own = outer_swap(mid_own)

    up_grad, gate_grad, partial_value = row_gradients(both, gate_pre, up_pre, gate_prob, row_token, block_expert)

    far_0, mid_near, x_1, y_1, out_own, partial_value, up_grad, gate_grad, piece_31, factor_near = together(
        far_0, mid_near, x_1, y_1, out_own, partial_value, up_grad, gate_grad, piece_31, factor_near
    )
    far_1 = sent((3, 1), piece_31)
    (far_1,) = stack_rows([[(far_1, 0, quarter)]], EARLY)
    to_x, to_y = stack_rows(
        [
            [(far_0, 0, quarter), (y_1, quarter, quarter)],
            [(far_0, 0, quarter), (x_1, 0, quarter)],
        ]
    )
    x_2, y_2 = along_x(to_x), along_y(to_y)
    out_near = outer_swap(mid_near)
    outer = (chip == 0) | (chip == chips - 1)
    factor_skip = jnp.where(outer, out_own, mid_near)
    near_factor = across(factor_near)

    far_1, x_2, y_2, out_near, near_factor, partial_value, factor_skip = together(
        far_1, x_2, y_2, out_near, near_factor, partial_value, factor_skip
    )
    to_x, to_y = stack_rows(
        [
            [(far_1, 0, quarter), (y_2, quarter // 2, quarter // 2)],
            [(far_1, 0, quarter), (x_2, 0, quarter // 2)],
        ]
    )
    x_3, y_3 = along_x(to_x), along_y(to_y)
    factor_far = jnp.where(outer, out_near, mid_own)
    skip_factor = across(factor_skip)
    far_factor = across(factor_far)
    partial_value = partial_value + along_x(partial_value)

    total = add_products(
        (own_tokens, other_tokens),
        ((0, 0, rows, 0), (1, 0, rows, rows)),
        factor,
        other_factor,
        jnp.zeros((share, EXPERTS * hidden_share), jnp.float32),
        rows,
    )

    def gathered(pairs, near, far, running, devices=0):
        parts, pieces = [], []
        for side, (own, x_hop, y_hop, row, diagonal) in enumerate(pairs):
            spot = side * rows
            base = len(parts)
            parts += [own, x_hop, y_hop] + [hop for hop, _, _ in diagonal]
            pieces += [
                (base, 0, quarter, spot),
                (base + 1, row, quarter, spot + quarter),
                (base + 2, row, quarter, spot + 2 * quarter),
            ]
            spot += 3 * quarter
            for index, (_, first, amount) in enumerate(diagonal):
                pieces.append((base + 3 + index, first, amount, spot))
                spot += amount
        return add_products(tuple(parts), tuple(pieces), near, far, running, rows, devices)

    half = quarter // 2
    total = gathered(
        (
            (near_0, x_0, y_0, 0, ((y_1, 2 * quarter, quarter),)),
            (near_1, x_1, y_1, 0, ((y_2, quarter, quarter),)),
        ),
        factor_near, near_factor, total,
    )
    total = gathered(
        (
            (skip_0, x_0, y_0, quarter, ((x_1, 2 * quarter, quarter),)),
            (skip_1, x_1, y_1, quarter, ((x_2, quarter, quarter),)),
        ),
        factor_skip, skip_factor, total,
    )

    x_3, y_3, total, partial_value, far_factor = together(x_3, y_3, total, partial_value, far_factor)
    prob_grad = (partial_value + along_y(partial_value))[0]
    x_4, y_4 = along_x(y_3[half:quarter]), along_y(x_3[:half])
    devices = columns * wide
    total, sums = gathered(
        (
            (far_0, x_2, y_2, 0, ((y_3, quarter, half), (x_3, quarter, half))),
            (far_1, x_3, y_3, 0, ((y_4, 0, half), (x_4, 0, half))),
        ),
        factor_far, far_factor, total, devices,
    )

    down_grad = total.reshape(share, EXPERTS, hidden_share)
    spread = lax.all_to_all(sums, ("blk", "wide"), 0, 0, tiled=True)
    total_sum = jnp.sum(spread, axis=0)[:EXPERTS]
    grad_rms = jnp.sqrt(total_sum / float(D * FFW))
    return (down_grad, grad_rms, prob_grad, gate_grad, up_grad)


def sums_body(upstream, gate_pre, up_pre, down_weight, block_expert, row_token, gate_prob):
    routed = upstream[row_token]
    row_count = routed.shape[0]
    block_count = row_count // BLOCK
    width = routed.shape[1]
    hidden_share = gate_pre.shape[1]
    gate_value = gate_pre.astype(jnp.float32)
    up_value = up_pre.astype(jnp.float32)
    sigmoid_gate = jax.nn.sigmoid(gate_value)
    active = gate_value * sigmoid_gate
    hidden = active * up_value
    weighted = (hidden * gate_prob[:, None]).astype(jnp.bfloat16)
    routed_blocks = routed.reshape(block_count, BLOCK, width)
    weighted_blocks = weighted.reshape(block_count, BLOCK, hidden_share)

    def project(block_item):
        rows_block, expert_id = block_item
        weights = lax.dynamic_index_in_dim(down_weight, expert_id, 1, keepdims=False)
        return jnp.dot(rows_block, weights, preferred_element_type=jnp.float32)

    projected = lax.map(project, (routed_blocks, block_expert)).reshape(row_count, hidden_share)
    scaled = gate_prob[:, None] * projected
    up_grad = (scaled * active).astype(jnp.bfloat16)
    gate_grad = (
        scaled * up_value * sigmoid_gate * (1.0 + gate_value * (1.0 - sigmoid_gate))
    ).astype(jnp.bfloat16)
    partial_value = jnp.sum(hidden * projected, axis=1)
    prob_grad = lax.psum(partial_value, "blk")
    row_share = width // lax.axis_size("wide")

    def select_columns(amount):
        return routed.reshape(block_count, BLOCK, amount)

    def block_product(columns, block_index):
        column_block = lax.dynamic_index_in_dim(columns, block_index, 0, keepdims=False)
        weighted_block = lax.dynamic_index_in_dim(weighted_blocks, block_index, 0, keepdims=False)
        return jnp.dot(column_block.T, weighted_block, preferred_element_type=jnp.float32)

    pieces = []
    for expert in range(EXPERTS):

        def one_expert(first, amount, expert=expert):
            columns = select_columns(amount)

            def add_block(block_index, running):
                expert_id = lax.dynamic_index_in_dim(block_expert, block_index, 0, keepdims=False)

                def with_block(running_sum):
                    return running_sum + block_product(columns, block_index)

                def without_block(running_sum):
                    return running_sum

                return lax.cond(expert_id == expert, with_block, without_block, running)

            start_value = jnp.zeros((amount, hidden_share), jnp.float32)
            return lax.fori_loop(0, block_count, add_block, start_value)

        pieces.append(
            lax.psum_scatter(
                one_expert(jnp.int32(0), lax.axis_size("wide") * row_share),
                "wide",
                scatter_dimension=0,
                tiled=True,
            )
        )
    down_grad = jnp.stack(pieces, axis=1)
    squares = jnp.sum(down_grad * down_grad, axis=(0, 2))
    total_sum = lax.psum(squares, ("blk", "wide"))
    grad_rms = jnp.sqrt(total_sum / float(D * FFW))
    return (down_grad, grad_rms, prob_grad, gate_grad, up_grad)


def solution(mesh):
    columns, wide = mesh.shape["blk"], mesh.shape["wide"]

    def body(upstream, gate_pre, up_pre, down_weight, block_expert, row_token, gate_prob):
        rows, width = upstream.shape
        hidden_share = gate_pre.shape[1]
        factors = wide * rows * (hidden_share + width // wide)
        sums = EXPERTS * width * hidden_share
        plan = factors_body if columns == 4 and wide == 8 and factors < sums else sums_body
        return plan(upstream, gate_pre, up_pre, down_weight, block_expert, row_token, gate_prob)

    in_specs = (
        P("wide", None),
        P("wide", "blk"),
        P("wide", "blk"),
        P(None, None, "blk"),
        P("wide"),
        P("wide"),
        P("wide"),
    )
    out_specs = (P("wide", None, "blk"), P(), P("wide"), P("wide", "blk"), P("wide", "blk"))
    return jax.shard_map(body, mesh=mesh, in_specs=in_specs, out_specs=out_specs, check_vma=False)
```

```python
import jax
import jax.numpy as jnp
from jax import lax
from jax.experimental import pallas as pl
from jax.experimental.pallas import tpu as pltpu
from jax.sharding import PartitionSpec as P

D = 7168
FFW = 1024
EXPERTS = 2
BLOCK = 128
VMEM = 56 * 1024 * 1024
EARLY = 20_000_000_000
LITTLE = 1_000_000_000
STACK_VMEM = 1024 * 1024


def add_products(parts, pieces, factors, total, rows, devices=0, token=None):
    share = parts[0].shape[-1]
    hidden_share = factors[0].shape[1]
    low = pieces[0][3]
    high = pieces[-1][3] + pieces[-1][2]
    last = () if token is None else (token,)
    n_parts, n_factors = len(parts), len(factors)

    def kernel(*refs):
        part_refs, factor_refs = refs[:n_parts], refs[n_parts : n_parts + n_factors]
        total_ref, out_ref = refs[n_parts + n_factors], refs[n_parts + n_factors + 1 + len(last)]
        left, right = refs[-2:]
        for part, first, amount, spot in pieces:
            left[spot - low : spot - low + amount, :] = part_refs[part][first : first + amount, :].astype(jnp.bfloat16)
        for side, factor_ref in enumerate(factor_refs):
            marks = factor_ref[rows:, :].T
            for first in range(0, rows, hidden_share):
                amount = min(hidden_share, rows - first)
                line = first // hidden_share
                begin = max(first, low - side * rows)
                end = min(first + amount, high - side * rows)
                if begin >= end:
                    continue
                mark = marks[begin - first : end - first, line : line + 1]
                weight = factor_ref[begin:end, :]
                spot = side * rows + begin - low
                for expert in range(EXPERTS):
                    right[spot : spot + end - begin, expert * hidden_share : (expert + 1) * hidden_share] = jnp.where(
                        mark == float(expert), weight, 0.0
                    ).astype(jnp.bfloat16)
        weights = right[...]
        squares = jnp.zeros((1, EXPERTS * hidden_share), jnp.float32)
        for first in range(0, share, 128):
            block = total_ref[first : first + 128, :] + lax.dot_general(
                left[:, first : first + 128],
                weights,
                (((0,), (0,)), ((), ())),
                preferred_element_type=jnp.float32,
            )
            out_ref[first : first + 128, :] = block
            if devices:
                squares = squares + jnp.sum(block * block, axis=0, keepdims=True)
        if devices:
            lane = lax.broadcasted_iota(jnp.int32, (devices, 128), 1)
            sums = jnp.zeros((devices, 128), jnp.float32)
            for expert in range(EXPERTS):
                own = squares[:, expert * hidden_share : (expert + 1) * hidden_share]
                sums = jnp.where(lane == expert, jnp.sum(own, axis=1, keepdims=True), sums)
            refs[-3][...] = sums

    depth = high - low
    out_shape = [jax.ShapeDtypeStruct(total.shape, jnp.float32)]
    if devices:
        out_shape.append(jax.ShapeDtypeStruct((devices, 128), jnp.float32))
    results = pl.pallas_call(
        kernel,
        out_shape=out_shape,
        in_specs=[pl.BlockSpec(memory_space=pltpu.VMEM)] * (n_parts + n_factors + 1)
        + [pl.BlockSpec(memory_space=pl.ANY)] * len(last),
        out_specs=[pl.BlockSpec(memory_space=pltpu.VMEM)] * len(out_shape),
        scratch_shapes=[
            pltpu.VMEM((depth, share), jnp.bfloat16),
            pltpu.VMEM((depth, EXPERTS * hidden_share), jnp.bfloat16),
        ],
        compiler_params=pltpu.CompilerParams(vmem_limit_bytes=16 * 1024 * 1024),
        cost_estimate=pl.CostEstimate(
            flops=2 * depth * share * EXPERTS * hidden_share,
            bytes_accessed=4 * depth * (share + hidden_share) + 8 * share * EXPERTS * hidden_share,
            transcendentals=0,
        ),
    )(*parts, *factors, total, *last)
    return results if devices else results[0]


def stack_rows(lists, flops=0):
    arrays = []
    for pieces in lists:
        for array, _, _ in pieces:
            if not any(array is one for one in arrays):
                arrays.append(array)
    places = [
        [([array is one for one in arrays].index(True), first, amount) for array, first, amount in pieces]
        for pieces in lists
    ]
    share = arrays[0].shape[1]
    heights = [sum(amount for _, _, amount in pieces) for pieces in lists]

    def kernel(*refs):
        for out_ref, pieces in zip(refs[len(arrays) :], places):
            spot = 0
            for index, first, amount in pieces:
                out_ref[spot : spot + amount, :] = refs[index][first : first + amount, :]
                spot += amount

    return pl.pallas_call(
        kernel,
        out_shape=[jax.ShapeDtypeStruct((height, share), jnp.float32) for height in heights],
        in_specs=[pl.BlockSpec(memory_space=pltpu.VMEM)] * len(arrays),
        out_specs=[pl.BlockSpec(memory_space=pltpu.VMEM)] * len(lists),
        compiler_params=pltpu.CompilerParams(vmem_limit_bytes=12 * 1024 * 1024),
        cost_estimate=pl.CostEstimate(flops=flops, bytes_accessed=8 * sum(heights) * share, transcendentals=0),
    )(*arrays)


def marker(values, flops):
    def kernel(*refs):
        refs[-1][...] = jnp.zeros_like(refs[-1])

    return pl.pallas_call(
        kernel,
        out_shape=jax.ShapeDtypeStruct((8, 128), jnp.float32),
        in_specs=[pl.BlockSpec(memory_space=pl.ANY)] * len(values),
        out_specs=pl.BlockSpec(memory_space=pltpu.VMEM),
        compiler_params=pltpu.CompilerParams(vmem_limit_bytes=1024 * 1024),
        cost_estimate=pl.CostEstimate(flops=flops, bytes_accessed=8192, transcendentals=0),
    )(*values)


def project(upstream, weights):
    rows, width = upstream.shape
    hidden_share = weights.shape[2]
    steps = 7 if width % (7 * 128) == 0 else 1
    block = width // steps

    def kernel(upstream_ref, weights_ref, out_ref):
        @pl.when(pl.program_id(0) == 0)
        def _():
            out_ref[...] = jnp.zeros_like(out_ref)

        for expert in range(EXPERTS):
            out_ref[expert] += jnp.dot(
                upstream_ref[...], weights_ref[expert], preferred_element_type=jnp.float32
            )

    return pl.pallas_call(
        kernel,
        out_shape=jax.ShapeDtypeStruct((EXPERTS, rows, hidden_share), jnp.float32),
        grid=(steps,),
        in_specs=[
            pl.BlockSpec((rows, block), lambda i: (0, i)),
            pl.BlockSpec((EXPERTS, block, hidden_share), lambda i: (0, i, 0)),
        ],
        out_specs=pl.BlockSpec((EXPERTS, rows, hidden_share), lambda i: (0, 0, 0)),
        compiler_params=pltpu.CompilerParams(vmem_limit_bytes=16 * 1024 * 1024),
        cost_estimate=pl.CostEstimate(
            flops=2 * rows * width * EXPERTS * hidden_share,
            bytes_accessed=2 * width * (rows + EXPERTS * hidden_share),
            transcendentals=0,
        ),
    )(upstream, weights)


def expert_line(expert_ref, rows):
    block = lax.broadcasted_iota(jnp.int32, (1, rows), 1) // BLOCK
    line = jnp.zeros((1, rows), jnp.float32)
    for index in range(rows // BLOCK):
        line = jnp.where(block == index, expert_ref[index].astype(jnp.float32), line)
    return line


def column_of(line):
    return jnp.broadcast_to(line, (8, line.shape[1])).T[:, :1]


def factor_of_tokens(gate_pre, up_pre, gate_prob, row_token, block_expert, blk_index, columns):
    rows, hidden_share = gate_pre.shape
    quarter = rows // columns

    def kernel(expert_ref, index_ref, gate_ref, up_ref, prob_ref, token_ref, out_ref):
        gate_value = gate_ref[...].astype(jnp.float32)
        hidden = gate_value * jax.nn.sigmoid(gate_value) * up_ref[...].astype(jnp.float32)
        weighted = (hidden * column_of(prob_ref[...].reshape(1, rows))).astype(jnp.bfloat16)
        place = lax.broadcasted_iota(jnp.int32, (rows, rows), 0)
        part = place // quarter
        token = (index_ref[0] ^ part) * quarter + (place - part * quarter)
        choose = jnp.where(token == token_ref[...].reshape(1, rows), 1.0, 0.0).astype(jnp.bfloat16)
        out_ref[:rows, :] = jnp.dot(choose, weighted, preferred_element_type=jnp.float32)
        experts = jnp.broadcast_to(expert_line(expert_ref, rows), (8, rows)).astype(jnp.bfloat16)
        marks = lax.dot_general(
            experts, choose, (((1,), (1,)), ((), ())), preferred_element_type=jnp.float32
        )
        out_ref[rows:, :] = jnp.zeros((8, hidden_share), jnp.float32)
        for first in range(0, rows, hidden_share):
            amount = min(hidden_share, rows - first)
            line = rows + first // hidden_share
            out_ref[line : line + 1, :amount] = marks[:1, first : first + amount]

    smem, vmem = pl.BlockSpec(memory_space=pltpu.SMEM), pl.BlockSpec(memory_space=pltpu.VMEM)
    return pl.pallas_call(
        kernel,
        out_shape=jax.ShapeDtypeStruct((rows + 8, hidden_share), jnp.float32),
        in_specs=[smem] * 2 + [vmem] * 4,
        out_specs=vmem,
        compiler_params=pltpu.CompilerParams(vmem_limit_bytes=VMEM),
        cost_estimate=pl.CostEstimate(flops=2 * rows * rows * hidden_share, bytes_accessed=12 * rows * hidden_share, transcendentals=0),
    )(block_expert, blk_index.reshape(1), gate_pre, up_pre, gate_prob, row_token)


def row_gradients(both, gate_pre, up_pre, gate_prob, row_token, block_expert):
    rows, hidden_share = gate_pre.shape

    def kernel(expert_ref, both_ref, gate_ref, up_ref, prob_ref, token_ref, up_grad_ref, gate_grad_ref, part_ref):
        place = lax.broadcasted_iota(jnp.int32, (rows, rows), 0)
        mine = place == token_ref[...].reshape(1, rows)
        expert_of_token = jnp.sum(jnp.where(mine, expert_line(expert_ref, rows), 0.0), axis=1, keepdims=True)
        of_token = both_ref[0]
        for expert in range(1, EXPERTS):
            of_token = jnp.where(expert_of_token == float(expert), both_ref[expert], of_token)
        choose = jnp.where(mine, 1.0, 0.0).astype(jnp.bfloat16)
        projected = jnp.zeros((rows, hidden_share), jnp.float32)
        rest = of_token
        for _ in range(3):
            top = rest.astype(jnp.bfloat16)
            projected = projected + lax.dot_general(
                choose, top, (((0,), (0,)), ((), ())), preferred_element_type=jnp.float32
            )
            rest = rest - top.astype(jnp.float32)
        gate_value = gate_ref[...].astype(jnp.float32)
        up_value = up_ref[...].astype(jnp.float32)
        sigmoid_gate = jax.nn.sigmoid(gate_value)
        active = gate_value * sigmoid_gate
        scaled = column_of(prob_ref[...].reshape(1, rows)) * projected
        up_grad_ref[...] = (scaled * active).astype(jnp.bfloat16)
        gate_grad_ref[...] = (
            scaled * up_value * sigmoid_gate * (1.0 + gate_value * (1.0 - sigmoid_gate))
        ).astype(jnp.bfloat16)
        part = jnp.sum(active * up_value * projected, axis=1, keepdims=True)
        part_ref[...] = jnp.broadcast_to(part, (rows, 128)).T[:8, :]

    smem, vmem = pl.BlockSpec(memory_space=pltpu.SMEM), pl.BlockSpec(memory_space=pltpu.VMEM)
    return pl.pallas_call(
        kernel,
        out_shape=[
            jax.ShapeDtypeStruct((rows, hidden_share), jnp.bfloat16),
            jax.ShapeDtypeStruct((rows, hidden_share), jnp.bfloat16),
            jax.ShapeDtypeStruct((8, rows), jnp.float32),
        ],
        in_specs=[smem] + [vmem] * 5,
        out_specs=[vmem] * 3,
        compiler_params=pltpu.CompilerParams(vmem_limit_bytes=16 * 1024 * 1024),
        cost_estimate=pl.CostEstimate(flops=6 * rows * rows * hidden_share, bytes_accessed=20 * rows * hidden_share, transcendentals=0),
    )(block_expert, both, gate_pre, up_pre, gate_prob, row_token)


def together(*values):
    return lax.optimization_barrier(values)


def factors_body(upstream, gate_pre, up_pre, down_weight, block_expert, row_token, gate_prob):
    rows, width = upstream.shape
    hidden_share = gate_pre.shape[1]
    columns = lax.axis_size("blk")
    wide = lax.axis_size("wide")
    chips = wide // 2
    quarter = rows // columns
    half = quarter // 2
    share = width // wide
    blk_index = lax.axis_index("blk")
    wide_index = lax.axis_index("wide")
    chip = wide_index // 2
    core = wide_index % 2

    def moved(value, target):
        pairs = []
        for b in range(columns):
            for z in range(chips):
                for c in range(2):
                    to = target(b, z, c)
                    pairs.append((b * wide + z * 2 + c, to[0] * wide + to[1] * 2 + to[2]))
        return lax.ppermute(value, ("blk", "wide"), pairs)

    def along_x(value):
        return moved(value, lambda b, z, c: (b ^ 1, z, c))

    def along_y(value):
        return moved(value, lambda b, z, c: (b ^ 2, z, c))

    def across(value):
        return moved(value, lambda b, z, c: (b, z, 1 - c))

    def outer_swap(value):
        return moved(value, lambda b, z, c: (b, z ^ 1, c))

    def middle_swap(value):
        return moved(value, lambda b, z, c: (b, 3 - z, c) if 0 < z < 3 else (b, z, 1 - c))

    def piece_for(key, index):
        offset, flip = key
        first_column = share * (2 * (chip ^ offset) + (core ^ flip))
        piece = lax.dynamic_slice(upstream, (quarter * index, first_column), (quarter, share))
        return piece.astype(jnp.float32)

    def sent(key, piece):
        offset, flip = key
        return moved(piece, lambda b, z, c: (b, z ^ offset, c ^ flip))

    near_0 = sent((1, 0), piece_for((1, 0), blk_index))
    skip_0 = sent((2, 0), piece_for((2, 0), blk_index))
    piece_11 = piece_for((1, 1), blk_index)
    factor = factor_of_tokens(gate_pre, up_pre, gate_prob, row_token, block_expert, blk_index, columns)
    factor_near = outer_swap(factor)
    mid_own = middle_swap(factor)
    other_factor = across(factor)

    def own_columns(of_core, index):
        first_column = share * (2 * chip + of_core)
        parts = [
            lax.dynamic_slice(upstream, (quarter * (index ^ q), first_column), (quarter, share))
            for q in range(columns)
        ]
        return jnp.concatenate(parts, axis=0).astype(jnp.float32)

    down_weight, index, _ = together(down_weight, blk_index, factor)
    weights = jnp.transpose(down_weight, (1, 0, 2))

    token = block_expert

    def arrive(*values, marked=(), flops=0):
        nonlocal token
        if marked:
            token = marker(marked + (token,), flops)
        *values, token = together(*values, token)
        return values

    half = quarter // 2

    near_0, skip_0, index, weights, piece_11 = arrive(near_0, skip_0, index, weights, piece_11)
    near_1 = sent((1, 1), piece_11)
    (spread,) = stack_rows([[(near_0, 0, quarter), (skip_0, 0, quarter)]], EARLY)
    x_0, y_0 = along_x(spread), along_y(spread)
    piece_21, piece_30, piece_31 = [piece_for(key, index) for key in ((2, 1), (3, 0), (3, 1))]
    own_tokens, other_tokens = own_columns(core, index), own_columns(1 - core, index)

    factor_near, mid_own, piece_21, piece_30, piece_31, other_tokens, other_factor = arrive(
        factor_near, mid_own, piece_21, piece_30, piece_31, other_tokens, other_factor,
        marked=(factor_near, mid_own, spread), flops=EARLY,
    )
    skip_1 = sent((2, 1), piece_21)

    x_0, y_0, near_1, mid_own = arrive(x_0, y_0, near_1, mid_own)
    to_x, to_y = stack_rows(
        [
            [(near_1, 0, quarter), (y_0, quarter, quarter)],
            [(near_1, 0, quarter), (x_0, 0, quarter)],
        ],
        EARLY,
    )
    x_1, y_1 = along_x(to_x), along_y(to_y)
    out_own = outer_swap(mid_own)

    skip_1, piece_30 = arrive(skip_1, piece_30, marked=(skip_1, to_x), flops=EARLY)
    far_0 = sent((3, 0), piece_30)

    x_1, y_1, other_tokens = arrive(x_1, y_1, other_tokens)
    to_x, to_y = stack_rows(
        [
            [(skip_1, 0, quarter), (y_1, half, half)],
            [(skip_1, 0, quarter), (x_1, 0, half)],
        ],
        EARLY,
    )
    x_2, y_2 = along_x(to_x), along_y(to_y)
    other_tokens = across(other_tokens)

    far_0, piece_31, weights = arrive(far_0, piece_31, weights, marked=(far_0, to_x), flops=EARLY)
    far_1 = sent((3, 1), piece_31)
    both = project(upstream, weights)

    x_2, y_2, factor_near, both, out_own, gate_pre = arrive(x_2, y_2, factor_near, both, out_own, gate_pre)
    to_x, to_y = stack_rows(
        [
            [(far_0, 0, quarter), (y_2, half, half)],
            [(far_0, 0, quarter), (x_2, 0, half)],
        ],
        EARLY,
    )
    x_3, y_3 = along_x(to_x), along_y(to_y)
    near_factor = across(factor_near)
    up_grad, gate_grad, partial_value = row_gradients(both, gate_pre, up_pre, gate_prob, row_token, block_expert)

    far_1, factor_near, partial_value, up_grad, gate_grad = arrive(
        far_1, factor_near, partial_value, up_grad, gate_grad, marked=(far_1, to_x), flops=EARLY
    )
    mid_near = middle_swap(factor_near)

    x_3, y_3, near_factor, partial_value, other_tokens = arrive(x_3, y_3, near_factor, partial_value, other_tokens)
    to_x, to_y = stack_rows(
        [
            [(far_1, 0, quarter), (y_3, half, half)],
            [(far_1, 0, quarter), (x_3, 0, half)],
        ],
        EARLY,
    )
    x_4, y_4 = along_x(to_x), along_y(to_y)
    partial_value = partial_value + along_x(partial_value)

    mid_near, mid_own, out_own = arrive(mid_near, mid_own, out_own, marked=(mid_near, to_x), flops=EARLY)
    out_near = outer_swap(mid_near)
    outer = (chip == 0) | (chip == chips - 1)
    factor_skip = jnp.where(outer, out_own, mid_near)
    skip_factor = across(factor_skip)

    def hopped(own, x_hop, y_hop, row, diagonal):
        parts = [own, x_hop, y_hop] + [hop for hop, _, _ in diagonal]
        pieces = [(0, 0, quarter, 0), (1, row, quarter, quarter), (2, row, quarter, 2 * quarter)]
        spot = 3 * quarter
        for index, (_, first, amount) in enumerate(diagonal):
            pieces.append((3 + index, first, amount, spot))
            spot += amount
        return parts, pieces

    def both_sides(one, two):
        shift = len(one[0])
        pieces = one[1] + [(part + shift, first, amount, spot + rows) for part, first, amount, spot in two[1]]
        return tuple(one[0] + two[0]), tuple(pieces)

    total = add_products(
        (own_tokens, other_tokens),
        ((0, 0, rows, 0), (1, 0, rows, rows)),
        (factor, other_factor),
        jnp.zeros((share, EXPERTS * hidden_share), jnp.float32),
        rows,
    )
    total = add_products(
        *both_sides(
            hopped(near_0, x_0, y_0, 0, ((y_1, quarter, quarter),)),
            hopped(near_1, x_1, y_1, 0, ((y_2, quarter, half), (x_2, quarter, half))),
        ),
        (factor_near, near_factor), total, rows,
    )
    total = add_products(
        *both_sides(
            hopped(skip_0, x_0, y_0, quarter, ((x_1, quarter, quarter),)),
            hopped(skip_1, x_2, y_2, 0, ((y_3, quarter, half), (x_3, quarter, half))),
        ),
        (factor_skip, skip_factor), total, rows,
    )

    x_4, y_4, partial_value = arrive(x_4, y_4, partial_value)
    to_x, to_y = stack_rows([[(y_4, half, half)], [(x_4, 0, half)]], LITTLE)
    x_5, y_5 = along_x(to_x), along_y(to_y)
    prob_grad = (partial_value + along_y(partial_value))[0]
    factor_far = jnp.where(outer, out_near, mid_own)
    far_factor = across(factor_far)
    parts, pieces = both_sides(
        hopped(far_0, x_3, y_3, 0, ((y_4, quarter, half), (x_4, quarter, half))),
        hopped(far_1, x_4, y_4, 0, ()),
    )
    total = add_products(parts, pieces, (factor_far, far_factor), total, rows)
    x_5, y_5 = arrive(x_5, y_5, marked=(x_5, y_5), flops=EARLY)
    devices = columns * wide
    total, sums = add_products(
        (y_5, x_5),
        ((0, 0, half, 3 * quarter), (1, 0, half, 3 * quarter + half)),
        (far_factor,), total, rows, devices, token,
    )

    down_grad = total.reshape(share, EXPERTS, hidden_share)
    spread = lax.all_to_all(sums, ("blk", "wide"), 0, 0, tiled=True)
    total_sum = jnp.sum(spread, axis=0)[:EXPERTS]
    grad_rms = jnp.sqrt(total_sum / float(D * FFW))
    return (down_grad, grad_rms, prob_grad, gate_grad, up_grad)


def sums_body(upstream, gate_pre, up_pre, down_weight, block_expert, row_token, gate_prob):
    routed = upstream[row_token]
    row_count = routed.shape[0]
    block_count = row_count // BLOCK
    width = routed.shape[1]
    hidden_share = gate_pre.shape[1]
    gate_value = gate_pre.astype(jnp.float32)
    up_value = up_pre.astype(jnp.float32)
    sigmoid_gate = jax.nn.sigmoid(gate_value)
    active = gate_value * sigmoid_gate
    hidden = active * up_value
    weighted = (hidden * gate_prob[:, None]).astype(jnp.bfloat16)
    routed_blocks = routed.reshape(block_count, BLOCK, width)
    weighted_blocks = weighted.reshape(block_count, BLOCK, hidden_share)

    def project(block_item):
        rows_block, expert_id = block_item
        weights = lax.dynamic_index_in_dim(down_weight, expert_id, 1, keepdims=False)
        return jnp.dot(rows_block, weights, preferred_element_type=jnp.float32)

    projected = lax.map(project, (routed_blocks, block_expert)).reshape(row_count, hidden_share)
    scaled = gate_prob[:, None] * projected
    up_grad = (scaled * active).astype(jnp.bfloat16)
    gate_grad = (
        scaled * up_value * sigmoid_gate * (1.0 + gate_value * (1.0 - sigmoid_gate))
    ).astype(jnp.bfloat16)
    partial_value = jnp.sum(hidden * projected, axis=1)
    prob_grad = lax.psum(partial_value, "blk")
    row_share = width // lax.axis_size("wide")

    def select_columns(amount):
        return routed.reshape(block_count, BLOCK, amount)

    def block_product(columns, block_index):
        column_block = lax.dynamic_index_in_dim(columns, block_index, 0, keepdims=False)
        weighted_block = lax.dynamic_index_in_dim(weighted_blocks, block_index, 0, keepdims=False)
        return jnp.dot(column_block.T, weighted_block, preferred_element_type=jnp.float32)

    pieces = []
    for expert in range(EXPERTS):

        def one_expert(first, amount, expert=expert):
            columns = select_columns(amount)

            def add_block(block_index, running):
                expert_id = lax.dynamic_index_in_dim(block_expert, block_index, 0, keepdims=False)

                def with_block(running_sum):
                    return running_sum + block_product(columns, block_index)

                def without_block(running_sum):
                    return running_sum

                return lax.cond(expert_id == expert, with_block, without_block, running)

            start_value = jnp.zeros((amount, hidden_share), jnp.float32)
            return lax.fori_loop(0, block_count, add_block, start_value)

        pieces.append(
            lax.psum_scatter(
                one_expert(jnp.int32(0), lax.axis_size("wide") * row_share),
                "wide",
                scatter_dimension=0,
                tiled=True,
            )
        )
    down_grad = jnp.stack(pieces, axis=1)
    squares = jnp.sum(down_grad * down_grad, axis=(0, 2))
    total_sum = lax.psum(squares, ("blk", "wide"))
    grad_rms = jnp.sqrt(total_sum / float(D * FFW))
    return (down_grad, grad_rms, prob_grad, gate_grad, up_grad)


def solution(mesh):
    columns, wide = mesh.shape["blk"], mesh.shape["wide"]

    def body(upstream, gate_pre, up_pre, down_weight, block_expert, row_token, gate_prob):
        rows, width = upstream.shape
        hidden_share = gate_pre.shape[1]
        factors = wide * rows * (hidden_share + width // wide)
        sums = EXPERTS * width * hidden_share
        plan = factors_body if columns == 4 and wide == 8 and factors < sums else sums_body
        return plan(upstream, gate_pre, up_pre, down_weight, block_expert, row_token, gate_prob)

    in_specs = (
        P("wide", None),
        P("wide", "blk"),
        P("wide", "blk"),
        P(None, None, "blk"),
        P("wide"),
        P("wide"),
        P("wide"),
    )
    out_specs = (P("wide", None, "blk"), P(), P("wide"), P("wide", "blk"), P("wide", "blk"))
    return jax.shard_map(body, mesh=mesh, in_specs=in_specs, out_specs=out_specs, check_vma=False)
```

```python
import jax
import jax.numpy as jnp
from jax import lax
from jax.experimental import pallas as pl
from jax.experimental.pallas import tpu as pltpu
from jax.sharding import PartitionSpec as P

D = 7168
FFW = 1024
EXPERTS = 2
BLOCK = 128
VMEM = 56 * 1024 * 1024
EARLY = 20_000_000_000
LITTLE = 1_000_000_000
STACK_VMEM = 1024 * 1024


def add_products(parts, pieces, factors, total, rows, devices=0, token=None):
    share = parts[0].shape[-1]
    hidden_share = factors[0].shape[1]
    low = pieces[0][3]
    high = pieces[-1][3] + pieces[-1][2]
    last = () if token is None else (token,)
    n_parts, n_factors = len(parts), len(factors)

    def kernel(*refs):
        part_refs, factor_refs = refs[:n_parts], refs[n_parts : n_parts + n_factors]
        total_ref, out_ref = refs[n_parts + n_factors], refs[n_parts + n_factors + 1 + len(last)]
        left, right = refs[-2:]
        for part, first, amount, spot in pieces:
            left[spot - low : spot - low + amount, :] = part_refs[part][first : first + amount, :].astype(jnp.bfloat16)
        for side, factor_ref in enumerate(factor_refs):
            marks = factor_ref[rows:, :].T
            for first in range(0, rows, hidden_share):
                amount = min(hidden_share, rows - first)
                line = first // hidden_share
                begin = max(first, low - side * rows)
                end = min(first + amount, high - side * rows)
                if begin >= end:
                    continue
                mark = marks[begin - first : end - first, line : line + 1]
                weight = factor_ref[begin:end, :]
                spot = side * rows + begin - low
                for expert in range(EXPERTS):
                    right[spot : spot + end - begin, expert * hidden_share : (expert + 1) * hidden_share] = jnp.where(
                        mark == float(expert), weight, 0.0
                    ).astype(jnp.bfloat16)
        weights = right[...]
        squares = jnp.zeros((1, EXPERTS * hidden_share), jnp.float32)
        for first in range(0, share, 128):
            block = total_ref[first : first + 128, :] + lax.dot_general(
                left[:, first : first + 128],
                weights,
                (((0,), (0,)), ((), ())),
                preferred_element_type=jnp.float32,
            )
            out_ref[first : first + 128, :] = block
            if devices:
                squares = squares + jnp.sum(block * block, axis=0, keepdims=True)
        if devices:
            lane = lax.broadcasted_iota(jnp.int32, (devices, 128), 1)
            sums = jnp.zeros((devices, 128), jnp.float32)
            for expert in range(EXPERTS):
                own = squares[:, expert * hidden_share : (expert + 1) * hidden_share]
                sums = jnp.where(lane == expert, jnp.sum(own, axis=1, keepdims=True), sums)
            refs[-3][...] = sums

    depth = high - low
    out_shape = [jax.ShapeDtypeStruct(total.shape, jnp.float32)]
    if devices:
        out_shape.append(jax.ShapeDtypeStruct((devices, 128), jnp.float32))
    results = pl.pallas_call(
        kernel,
        out_shape=out_shape,
        in_specs=[pl.BlockSpec(memory_space=pltpu.VMEM)] * (n_parts + n_factors + 1)
        + [pl.BlockSpec(memory_space=pl.ANY)] * len(last),
        out_specs=[pl.BlockSpec(memory_space=pltpu.VMEM)] * len(out_shape),
        scratch_shapes=[
            pltpu.VMEM((depth, share), jnp.bfloat16),
            pltpu.VMEM((depth, EXPERTS * hidden_share), jnp.bfloat16),
        ],
        compiler_params=pltpu.CompilerParams(vmem_limit_bytes=16 * 1024 * 1024),
        cost_estimate=pl.CostEstimate(
            flops=2 * depth * share * EXPERTS * hidden_share,
            bytes_accessed=4 * depth * (share + hidden_share) + 8 * share * EXPERTS * hidden_share,
            transcendentals=0,
        ),
    )(*parts, *factors, total, *last)
    return results if devices else results[0]


def stack_rows(lists, flops=0):
    arrays = []
    for pieces in lists:
        for array, _, _ in pieces:
            if not any(array is one for one in arrays):
                arrays.append(array)
    places = [
        [([array is one for one in arrays].index(True), first, amount) for array, first, amount in pieces]
        for pieces in lists
    ]
    share = arrays[0].shape[1]
    heights = [sum(amount for _, _, amount in pieces) for pieces in lists]

    def kernel(*refs):
        for out_ref, pieces in zip(refs[len(arrays) :], places):
            spot = 0
            for index, first, amount in pieces:
                out_ref[spot : spot + amount, :] = refs[index][first : first + amount, :]
                spot += amount

    return pl.pallas_call(
        kernel,
        out_shape=[jax.ShapeDtypeStruct((height, share), jnp.float32) for height in heights],
        in_specs=[pl.BlockSpec(memory_space=pltpu.VMEM)] * len(arrays),
        out_specs=[pl.BlockSpec(memory_space=pltpu.VMEM)] * len(lists),
        compiler_params=pltpu.CompilerParams(vmem_limit_bytes=12 * 1024 * 1024),
        cost_estimate=pl.CostEstimate(flops=flops, bytes_accessed=8 * sum(heights) * share, transcendentals=0),
    )(*arrays)


def marker(values, flops):
    def kernel(*refs):
        refs[-1][...] = jnp.zeros_like(refs[-1])

    return pl.pallas_call(
        kernel,
        out_shape=jax.ShapeDtypeStruct((8, 128), jnp.float32),
        in_specs=[pl.BlockSpec(memory_space=pl.ANY)] * len(values),
        out_specs=pl.BlockSpec(memory_space=pltpu.VMEM),
        compiler_params=pltpu.CompilerParams(vmem_limit_bytes=1024 * 1024),
        cost_estimate=pl.CostEstimate(flops=flops, bytes_accessed=8192, transcendentals=0),
    )(*values)


def project(upstream, weights):
    rows, width = upstream.shape
    hidden_share = weights.shape[2]
    steps = 7 if width % (7 * 128) == 0 else 1
    block = width // steps

    def kernel(upstream_ref, weights_ref, out_ref):
        @pl.when(pl.program_id(0) == 0)
        def _():
            out_ref[...] = jnp.zeros_like(out_ref)

        for expert in range(EXPERTS):
            out_ref[expert] += jnp.dot(
                upstream_ref[...], weights_ref[expert], preferred_element_type=jnp.float32
            )

    return pl.pallas_call(
        kernel,
        out_shape=jax.ShapeDtypeStruct((EXPERTS, rows, hidden_share), jnp.float32),
        grid=(steps,),
        in_specs=[
            pl.BlockSpec((rows, block), lambda i: (0, i)),
            pl.BlockSpec((EXPERTS, block, hidden_share), lambda i: (0, i, 0)),
        ],
        out_specs=pl.BlockSpec((EXPERTS, rows, hidden_share), lambda i: (0, 0, 0)),
        compiler_params=pltpu.CompilerParams(vmem_limit_bytes=16 * 1024 * 1024),
        cost_estimate=pl.CostEstimate(
            flops=2 * rows * width * EXPERTS * hidden_share,
            bytes_accessed=2 * width * (rows + EXPERTS * hidden_share),
            transcendentals=0,
        ),
    )(upstream, weights)


def expert_line(expert_ref, rows):
    block = lax.broadcasted_iota(jnp.int32, (1, rows), 1) // BLOCK
    line = jnp.zeros((1, rows), jnp.float32)
    for index in range(rows // BLOCK):
        line = jnp.where(block == index, expert_ref[index].astype(jnp.float32), line)
    return line


def column_of(line):
    return jnp.broadcast_to(line, (8, line.shape[1])).T[:, :1]


def factor_of_tokens(gate_pre, up_pre, gate_prob, row_token, block_expert, blk_index, columns):
    rows, hidden_share = gate_pre.shape
    quarter = rows // columns

    def kernel(expert_ref, index_ref, gate_ref, up_ref, prob_ref, token_ref, out_ref):
        gate_value = gate_ref[...].astype(jnp.float32)
        hidden = gate_value * jax.nn.sigmoid(gate_value) * up_ref[...].astype(jnp.float32)
        weighted = (hidden * column_of(prob_ref[...].reshape(1, rows))).astype(jnp.bfloat16)
        place = lax.broadcasted_iota(jnp.int32, (rows, rows), 0)
        part = place // quarter
        token = (index_ref[0] ^ part) * quarter + (place - part * quarter)
        choose = jnp.where(token == token_ref[...].reshape(1, rows), 1.0, 0.0).astype(jnp.bfloat16)
        out_ref[:rows, :] = jnp.dot(choose, weighted, preferred_element_type=jnp.float32)
        experts = jnp.broadcast_to(expert_line(expert_ref, rows), (8, rows)).astype(jnp.bfloat16)
        marks = lax.dot_general(
            experts, choose, (((1,), (1,)), ((), ())), preferred_element_type=jnp.float32
        )
        out_ref[rows:, :] = jnp.zeros((8, hidden_share), jnp.float32)
        for first in range(0, rows, hidden_share):
            amount = min(hidden_share, rows - first)
            line = rows + first // hidden_share
            out_ref[line : line + 1, :amount] = marks[:1, first : first + amount]

    smem, vmem = pl.BlockSpec(memory_space=pltpu.SMEM), pl.BlockSpec(memory_space=pltpu.VMEM)
    return pl.pallas_call(
        kernel,
        out_shape=jax.ShapeDtypeStruct((rows + 8, hidden_share), jnp.float32),
        in_specs=[smem] * 2 + [vmem] * 4,
        out_specs=vmem,
        compiler_params=pltpu.CompilerParams(vmem_limit_bytes=VMEM),
        cost_estimate=pl.CostEstimate(flops=2 * rows * rows * hidden_share, bytes_accessed=12 * rows * hidden_share, transcendentals=0),
    )(block_expert, blk_index.reshape(1), gate_pre, up_pre, gate_prob, row_token)


def row_gradients(both, gate_pre, up_pre, gate_prob, row_token, block_expert):
    rows, hidden_share = gate_pre.shape

    def kernel(expert_ref, both_ref, gate_ref, up_ref, prob_ref, token_ref, up_grad_ref, gate_grad_ref, part_ref):
        place = lax.broadcasted_iota(jnp.int32, (rows, rows), 0)
        mine = place == token_ref[...].reshape(1, rows)
        expert_of_token = jnp.sum(jnp.where(mine, expert_line(expert_ref, rows), 0.0), axis=1, keepdims=True)
        of_token = both_ref[0]
        for expert in range(1, EXPERTS):
            of_token = jnp.where(expert_of_token == float(expert), both_ref[expert], of_token)
        choose = jnp.where(mine, 1.0, 0.0).astype(jnp.bfloat16)
        projected = jnp.zeros((rows, hidden_share), jnp.float32)
        rest = of_token
        for _ in range(3):
            top = rest.astype(jnp.bfloat16)
            projected = projected + lax.dot_general(
                choose, top, (((0,), (0,)), ((), ())), preferred_element_type=jnp.float32
            )
            rest = rest - top.astype(jnp.float32)
        gate_value = gate_ref[...].astype(jnp.float32)
        up_value = up_ref[...].astype(jnp.float32)
        sigmoid_gate = jax.nn.sigmoid(gate_value)
        active = gate_value * sigmoid_gate
        scaled = column_of(prob_ref[...].reshape(1, rows)) * projected
        up_grad_ref[...] = (scaled * active).astype(jnp.bfloat16)
        gate_grad_ref[...] = (
            scaled * up_value * sigmoid_gate * (1.0 + gate_value * (1.0 - sigmoid_gate))
        ).astype(jnp.bfloat16)
        part = jnp.sum(active * up_value * projected, axis=1, keepdims=True)
        part_ref[...] = jnp.broadcast_to(part, (rows, 128)).T[:8, :]

    smem, vmem = pl.BlockSpec(memory_space=pltpu.SMEM), pl.BlockSpec(memory_space=pltpu.VMEM)
    return pl.pallas_call(
        kernel,
        out_shape=[
            jax.ShapeDtypeStruct((rows, hidden_share), jnp.bfloat16),
            jax.ShapeDtypeStruct((rows, hidden_share), jnp.bfloat16),
            jax.ShapeDtypeStruct((8, rows), jnp.float32),
        ],
        in_specs=[smem] + [vmem] * 5,
        out_specs=[vmem] * 3,
        compiler_params=pltpu.CompilerParams(vmem_limit_bytes=16 * 1024 * 1024),
        cost_estimate=pl.CostEstimate(flops=6 * rows * rows * hidden_share, bytes_accessed=20 * rows * hidden_share, transcendentals=0),
    )(block_expert, both, gate_pre, up_pre, gate_prob, row_token)


def together(*values):
    return lax.optimization_barrier(values)


def factors_body(upstream, gate_pre, up_pre, down_weight, block_expert, row_token, gate_prob):
    rows, width = upstream.shape
    hidden_share = gate_pre.shape[1]
    columns = lax.axis_size("blk")
    wide = lax.axis_size("wide")
    chips = wide // 2
    quarter = rows // columns
    half = quarter // 2
    share = width // wide
    blk_index = lax.axis_index("blk")
    wide_index = lax.axis_index("wide")
    chip = wide_index // 2
    core = wide_index % 2

    def moved(value, target):
        pairs = []
        for b in range(columns):
            for z in range(chips):
                for c in range(2):
                    to = target(b, z, c)
                    pairs.append((b * wide + z * 2 + c, to[0] * wide + to[1] * 2 + to[2]))
        return lax.ppermute(value, ("blk", "wide"), pairs)

    def along_x(value):
        return moved(value, lambda b, z, c: (b ^ 1, z, c))

    def along_y(value):
        return moved(value, lambda b, z, c: (b ^ 2, z, c))

    def across(value):
        return moved(value, lambda b, z, c: (b, z, 1 - c))

    def outer_swap(value):
        return moved(value, lambda b, z, c: (b, z ^ 1, c))

    def middle_swap(value):
        return moved(value, lambda b, z, c: (b, 3 - z, c) if 0 < z < 3 else (b, z, 1 - c))

    def piece_for(key, index):
        offset, flip = key
        first_column = share * (2 * (chip ^ offset) + (core ^ flip))
        piece = lax.dynamic_slice(upstream, (quarter * index, first_column), (quarter, share))
        return piece.astype(jnp.float32)

    def sent(key, piece):
        offset, flip = key
        return moved(piece, lambda b, z, c: (b, z ^ offset, c ^ flip))

    near_0 = sent((1, 0), piece_for((1, 0), blk_index))
    skip_0 = sent((2, 0), piece_for((2, 0), blk_index))
    piece_11, piece_21 = piece_for((1, 1), blk_index), piece_for((2, 1), blk_index)
    factor = factor_of_tokens(gate_pre, up_pre, gate_prob, row_token, block_expert, blk_index, columns)
    mid_own = middle_swap(factor)
    other_factor = across(factor)

    def own_columns(of_core, index):
        first_column = share * (2 * chip + of_core)
        parts = [
            lax.dynamic_slice(upstream, (quarter * (index ^ q), first_column), (quarter, share))
            for q in range(columns)
        ]
        return jnp.concatenate(parts, axis=0).astype(jnp.float32)

    down_weight, index, _ = together(down_weight, blk_index, factor)
    weights = jnp.transpose(down_weight, (1, 0, 2))

    token = None

    def arrive(*values, marked=(), flops=0):
        nonlocal token
        if marked:
            token = marker(marked + (() if token is None else (token,)), flops)
        if token is None:
            return together(*values) if len(values) > 1 else values
        *values, token = together(*values, token)
        return values

    half = quarter // 2

    near_0, skip_0, index, weights, piece_11 = arrive(near_0, skip_0, index, weights, piece_11)
    near_1 = sent((1, 1), piece_11)
    (spread,) = stack_rows([[(near_0, 0, quarter), (skip_0, 0, quarter)]], EARLY)
    sent_0 = spread
    x_0, y_0 = along_x(spread), along_y(spread)

    mid_own, factor, piece_21, other_factor, index = arrive(
        mid_own, factor, piece_21, other_factor, index, marked=(mid_own, spread), flops=EARLY
    )
    piece_30, piece_31 = [piece_for(key, index) for key in ((3, 0), (3, 1))]
    own_tokens, other_tokens = own_columns(core, index), own_columns(1 - core, index)
    skip_1 = sent((2, 1), piece_21)

    x_0, y_0, near_1, piece_30, piece_31, other_tokens, own_tokens = arrive(
        x_0, y_0, near_1, piece_30, piece_31, other_tokens, own_tokens
    )
    to_x, to_y = stack_rows(
        [
            [(near_1, 0, quarter), (y_0, quarter, quarter)],
            [(near_1, 0, quarter), (x_0, 0, quarter)],
        ],
        EARLY,
    )
    sent_1 = to_x
    x_1, y_1 = along_x(to_x), along_y(to_y)

    skip_1, piece_30, factor, weights = arrive(
        skip_1, piece_30, factor, weights, marked=(skip_1, to_x), flops=EARLY
    )
    far_0 = sent((3, 0), piece_30)
    both = project(upstream, weights)

    x_1, y_1, other_tokens, both, factor = arrive(x_1, y_1, other_tokens, both, factor)
    factor_near = outer_swap(factor)
    to_x, to_y = stack_rows(
        [
            [(skip_1, 0, quarter), (y_1, half, half)],
            [(skip_1, 0, quarter), (x_1, 0, half)],
        ],
        EARLY,
    )
    sent_2 = to_x
    x_2, y_2 = along_x(to_x), along_y(to_y)
    other_tokens = across(other_tokens)

    far_0, piece_31, mid_own = arrive(far_0, piece_31, mid_own, marked=(far_0, to_x), flops=EARLY)
    far_1 = sent((3, 1), piece_31)
    out_own = outer_swap(mid_own)

    x_2, y_2, factor_near, other_tokens = arrive(x_2, y_2, factor_near, other_tokens)
    to_x, to_y = stack_rows(
        [
            [(far_0, 0, quarter), (y_2, half, half)],
            [(far_0, 0, quarter), (x_2, 0, half)],
        ],
        EARLY,
    )
    sent_3 = to_x
    x_3, y_3 = along_x(to_x), along_y(to_y)
    near_factor = across(factor_near)

    far_1, factor_near, gate_pre = arrive(far_1, factor_near, gate_pre, marked=(far_1, to_x), flops=EARLY)
    mid_near = middle_swap(factor_near)
    up_grad, gate_grad, partial_value = row_gradients(both, gate_pre, up_pre, gate_prob, row_token, block_expert)

    x_3, y_3, near_factor, partial_value, up_grad, gate_grad = arrive(
        x_3, y_3, near_factor, partial_value, up_grad, gate_grad
    )
    to_x, to_y = stack_rows(
        [
            [(far_1, 0, quarter), (y_3, half, half)],
            [(far_1, 0, quarter), (x_3, 0, half)],
        ],
        EARLY,
    )
    sent_4 = to_x
    x_4, y_4 = along_x(to_x), along_y(to_y)
    partial_value = partial_value + along_x(partial_value)

    mid_near, mid_own, out_own = arrive(mid_near, mid_own, out_own, marked=(mid_near, to_x), flops=EARLY)
    out_near = outer_swap(mid_near)
    outer = (chip == 0) | (chip == chips - 1)
    factor_skip = jnp.where(outer, out_own, mid_near)
    skip_factor = across(factor_skip)

    def hopped(own, own_row, x_hop, y_hop, row, diagonal):
        parts = [own, x_hop, y_hop] + [hop for hop, _, _ in diagonal]
        pieces = [(0, own_row, quarter, 0), (1, row, quarter, quarter), (2, row, quarter, 2 * quarter)]
        spot = 3 * quarter
        for index, (_, first, amount) in enumerate(diagonal):
            pieces.append((3 + index, first, amount, spot))
            spot += amount
        return parts, pieces

    def both_sides(one, two):
        shift = len(one[0])
        pieces = one[1] + [(part + shift, first, amount, spot + rows) for part, first, amount, spot in two[1]]
        return tuple(one[0] + two[0]), tuple(pieces)

    total = add_products(
        (own_tokens, other_tokens),
        ((0, 0, rows, 0), (1, 0, rows, rows)),
        (factor, other_factor),
        jnp.zeros((share, EXPERTS * hidden_share), jnp.float32),
        rows,
    )
    total = add_products(
        *both_sides(
            hopped(sent_0, 0, x_0, y_0, 0, ((y_1, quarter, quarter),)),
            hopped(sent_1, 0, x_1, y_1, 0, ((y_2, quarter, half), (x_2, quarter, half))),
        ),
        (factor_near, near_factor), total, rows,
    )
    total = add_products(
        *both_sides(
            hopped(sent_0, quarter, x_0, y_0, quarter, ((x_1, quarter, quarter),)),
            hopped(sent_2, 0, x_2, y_2, 0, ((y_3, quarter, half), (x_3, quarter, half))),
        ),
        (factor_skip, skip_factor), total, rows,
    )

    x_4, y_4, partial_value = arrive(x_4, y_4, partial_value)
    to_x, to_y = stack_rows([[(y_4, half, half)], [(x_4, 0, half)]], LITTLE)
    x_5, y_5 = along_x(to_x), along_y(to_y)
    prob_grad = (partial_value + along_y(partial_value))[0]
    factor_far = jnp.where(outer, out_near, mid_own)
    far_factor = across(factor_far)
    parts, pieces = both_sides(
        hopped(sent_3, 0, x_3, y_3, 0, ((y_4, quarter, half), (x_4, quarter, half))),
        hopped(sent_4, 0, x_4, y_4, 0, ()),
    )
    total = add_products(parts, pieces, (factor_far, far_factor), total, rows)
    x_5, y_5 = arrive(x_5, y_5, marked=(x_5, y_5), flops=EARLY)
    devices = columns * wide
    total, sums = add_products(
        (y_5, x_5),
        ((0, 0, half, 3 * quarter), (1, 0, half, 3 * quarter + half)),
        (far_factor,), total, rows, devices, token,
    )

    down_grad = total.reshape(share, EXPERTS, hidden_share)
    spread = lax.all_to_all(sums, ("blk", "wide"), 0, 0, tiled=True)
    total_sum = jnp.sum(spread, axis=0)[:EXPERTS]
    grad_rms = jnp.sqrt(total_sum / float(D * FFW))
    return (down_grad, grad_rms, prob_grad, gate_grad, up_grad)


def sums_body(upstream, gate_pre, up_pre, down_weight, block_expert, row_token, gate_prob):
    routed = upstream[row_token]
    row_count = routed.shape[0]
    block_count = row_count // BLOCK
    width = routed.shape[1]
    hidden_share = gate_pre.shape[1]
    gate_value = gate_pre.astype(jnp.float32)
    up_value = up_pre.astype(jnp.float32)
    sigmoid_gate = jax.nn.sigmoid(gate_value)
    active = gate_value * sigmoid_gate
    hidden = active * up_value
    weighted = (hidden * gate_prob[:, None]).astype(jnp.bfloat16)
    routed_blocks = routed.reshape(block_count, BLOCK, width)
    weighted_blocks = weighted.reshape(block_count, BLOCK, hidden_share)

    def project(block_item):
        rows_block, expert_id = block_item
        weights = lax.dynamic_index_in_dim(down_weight, expert_id, 1, keepdims=False)
        return jnp.dot(rows_block, weights, preferred_element_type=jnp.float32)

    projected = lax.map(project, (routed_blocks, block_expert)).reshape(row_count, hidden_share)
    scaled = gate_prob[:, None] * projected
    up_grad = (scaled * active).astype(jnp.bfloat16)
    gate_grad = (
        scaled * up_value * sigmoid_gate * (1.0 + gate_value * (1.0 - sigmoid_gate))
    ).astype(jnp.bfloat16)
    partial_value = jnp.sum(hidden * projected, axis=1)
    prob_grad = lax.psum(partial_value, "blk")
    row_share = width // lax.axis_size("wide")

    def select_columns(amount):
        return routed.reshape(block_count, BLOCK, amount)

    def block_product(columns, block_index):
        column_block = lax.dynamic_index_in_dim(columns, block_index, 0, keepdims=False)
        weighted_block = lax.dynamic_index_in_dim(weighted_blocks, block_index, 0, keepdims=False)
        return jnp.dot(column_block.T, weighted_block, preferred_element_type=jnp.float32)

    pieces = []
    for expert in range(EXPERTS):

        def one_expert(first, amount, expert=expert):
            columns = select_columns(amount)

            def add_block(block_index, running):
                expert_id = lax.dynamic_index_in_dim(block_expert, block_index, 0, keepdims=False)

                def with_block(running_sum):
                    return running_sum + block_product(columns, block_index)

                def without_block(running_sum):
                    return running_sum

                return lax.cond(expert_id == expert, with_block, without_block, running)

            start_value = jnp.zeros((amount, hidden_share), jnp.float32)
            return lax.fori_loop(0, block_count, add_block, start_value)

        pieces.append(
            lax.psum_scatter(
                one_expert(jnp.int32(0), lax.axis_size("wide") * row_share),
                "wide",
                scatter_dimension=0,
                tiled=True,
            )
        )
    down_grad = jnp.stack(pieces, axis=1)
    squares = jnp.sum(down_grad * down_grad, axis=(0, 2))
    total_sum = lax.psum(squares, ("blk", "wide"))
    grad_rms = jnp.sqrt(total_sum / float(D * FFW))
    return (down_grad, grad_rms, prob_grad, gate_grad, up_grad)


def solution(mesh):
    columns, wide = mesh.shape["blk"], mesh.shape["wide"]

    def body(upstream, gate_pre, up_pre, down_weight, block_expert, row_token, gate_prob):
        rows, width = upstream.shape
        hidden_share = gate_pre.shape[1]
        factors = wide * rows * (hidden_share + width // wide)
        sums = EXPERTS * width * hidden_share
        plan = factors_body if columns == 4 and wide == 8 and factors < sums else sums_body
        return plan(upstream, gate_pre, up_pre, down_weight, block_expert, row_token, gate_prob)

    in_specs = (
        P("wide", None),
        P("wide", "blk"),
        P("wide", "blk"),
        P(None, None, "blk"),
        P("wide"),
        P("wide"),
        P("wide"),
    )
    out_specs = (P("wide", None, "blk"), P(), P("wide"), P("wide", "blk"), P("wide", "blk"))
    return jax.shard_map(body, mesh=mesh, in_specs=in_specs, out_specs=out_specs, check_vma=False)
```

```python
import jax
import jax.numpy as jnp
from jax import lax
from jax.experimental import pallas as pl
from jax.experimental.pallas import tpu as pltpu
from jax.sharding import PartitionSpec as P

D = 7168
FFW = 1024
EXPERTS = 2
BLOCK = 128
VMEM = 56 * 1024 * 1024
EARLY = 20_000_000_000
LITTLE = 1_000_000_000
STACK_VMEM = 1024 * 1024


def add_products(parts, pieces, factors, total, rows, devices=0, token=None):
    share = parts[0].shape[-1]
    hidden_share = factors[0].shape[1]
    low = pieces[0][3]
    high = pieces[-1][3] + pieces[-1][2]
    last = () if token is None else (token,)
    n_parts, n_factors = len(parts), len(factors)

    def kernel(*refs):
        part_refs, factor_refs = refs[:n_parts], refs[n_parts : n_parts + n_factors]
        total_ref, out_ref = refs[n_parts + n_factors], refs[n_parts + n_factors + 1 + len(last)]
        left, right = refs[-2:]
        for part, first, amount, spot in pieces:
            left[spot - low : spot - low + amount, :] = part_refs[part][first : first + amount, :].astype(jnp.bfloat16)
        for side, factor_ref in enumerate(factor_refs):
            marks = factor_ref[rows:, :].T
            for first in range(0, rows, hidden_share):
                amount = min(hidden_share, rows - first)
                line = first // hidden_share
                begin = max(first, low - side * rows)
                end = min(first + amount, high - side * rows)
                if begin >= end:
                    continue
                mark = marks[begin - first : end - first, line : line + 1]
                weight = factor_ref[begin:end, :]
                spot = side * rows + begin - low
                for expert in range(EXPERTS):
                    right[spot : spot + end - begin, expert * hidden_share : (expert + 1) * hidden_share] = jnp.where(
                        mark == float(expert), weight, 0.0
                    ).astype(jnp.bfloat16)
        weights = right[...]
        squares = jnp.zeros((1, EXPERTS * hidden_share), jnp.float32)
        for first in range(0, share, 128):
            block = total_ref[first : first + 128, :] + lax.dot_general(
                left[:, first : first + 128],
                weights,
                (((0,), (0,)), ((), ())),
                preferred_element_type=jnp.float32,
            )
            out_ref[first : first + 128, :] = block
            if devices:
                squares = squares + jnp.sum(block * block, axis=0, keepdims=True)
        if devices:
            lane = lax.broadcasted_iota(jnp.int32, (devices, 128), 1)
            sums = jnp.zeros((devices, 128), jnp.float32)
            for expert in range(EXPERTS):
                own = squares[:, expert * hidden_share : (expert + 1) * hidden_share]
                sums = jnp.where(lane == expert, jnp.sum(own, axis=1, keepdims=True), sums)
            refs[-3][...] = sums

    depth = high - low
    out_shape = [jax.ShapeDtypeStruct(total.shape, jnp.float32)]
    if devices:
        out_shape.append(jax.ShapeDtypeStruct((devices, 128), jnp.float32))
    results = pl.pallas_call(
        kernel,
        out_shape=out_shape,
        in_specs=[pl.BlockSpec(memory_space=pltpu.VMEM)] * (n_parts + n_factors + 1)
        + [pl.BlockSpec(memory_space=pl.ANY)] * len(last),
        out_specs=[pl.BlockSpec(memory_space=pltpu.VMEM)] * len(out_shape),
        scratch_shapes=[
            pltpu.VMEM((depth, share), jnp.bfloat16),
            pltpu.VMEM((depth, EXPERTS * hidden_share), jnp.bfloat16),
        ],
        compiler_params=pltpu.CompilerParams(vmem_limit_bytes=16 * 1024 * 1024),
        cost_estimate=pl.CostEstimate(
            flops=2 * depth * share * EXPERTS * hidden_share,
            bytes_accessed=4 * depth * (share + hidden_share) + 8 * share * EXPERTS * hidden_share,
            transcendentals=0,
        ),
    )(*parts, *factors, total, *last)
    return results if devices else results[0]


def stack_rows(lists, flops=0):
    arrays = []
    for pieces in lists:
        for array, _, _ in pieces:
            if not any(array is one for one in arrays):
                arrays.append(array)
    places = [
        [([array is one for one in arrays].index(True), first, amount) for array, first, amount in pieces]
        for pieces in lists
    ]
    share = arrays[0].shape[1]
    heights = [sum(amount for _, _, amount in pieces) for pieces in lists]

    def kernel(*refs):
        for out_ref, pieces in zip(refs[len(arrays) :], places):
            spot = 0
            for index, first, amount in pieces:
                out_ref[spot : spot + amount, :] = refs[index][first : first + amount, :]
                spot += amount

    return pl.pallas_call(
        kernel,
        out_shape=[jax.ShapeDtypeStruct((height, share), jnp.float32) for height in heights],
        in_specs=[pl.BlockSpec(memory_space=pltpu.VMEM)] * len(arrays),
        out_specs=[pl.BlockSpec(memory_space=pltpu.VMEM)] * len(lists),
        compiler_params=pltpu.CompilerParams(vmem_limit_bytes=12 * 1024 * 1024),
        cost_estimate=pl.CostEstimate(flops=flops, bytes_accessed=8 * sum(heights) * share, transcendentals=0),
    )(*arrays)


def marker(values, flops):
    def kernel(*refs):
        refs[-1][...] = jnp.zeros_like(refs[-1])

    return pl.pallas_call(
        kernel,
        out_shape=jax.ShapeDtypeStruct((8, 128), jnp.float32),
        in_specs=[pl.BlockSpec(memory_space=pl.ANY)] * len(values),
        out_specs=pl.BlockSpec(memory_space=pltpu.VMEM),
        compiler_params=pltpu.CompilerParams(vmem_limit_bytes=1024 * 1024),
        cost_estimate=pl.CostEstimate(flops=flops, bytes_accessed=8192, transcendentals=0),
    )(*values)


def project(upstream, weights):
    rows, width = upstream.shape
    hidden_share = weights.shape[2]
    steps = 4 if width % (4 * 128) == 0 else 1
    block = width // steps

    def kernel(upstream_ref, weights_ref, out_ref):
        @pl.when(pl.program_id(0) == 0)
        def _():
            out_ref[...] = jnp.zeros_like(out_ref)

        for expert in range(EXPERTS):
            out_ref[expert] += jnp.dot(
                upstream_ref[...], weights_ref[expert], preferred_element_type=jnp.float32
            )

    return pl.pallas_call(
        kernel,
        out_shape=jax.ShapeDtypeStruct((EXPERTS, rows, hidden_share), jnp.float32),
        grid=(steps,),
        in_specs=[
            pl.BlockSpec((rows, block), lambda i: (0, i)),
            pl.BlockSpec((EXPERTS, block, hidden_share), lambda i: (0, i, 0)),
        ],
        out_specs=pl.BlockSpec((EXPERTS, rows, hidden_share), lambda i: (0, 0, 0)),
        compiler_params=pltpu.CompilerParams(vmem_limit_bytes=16 * 1024 * 1024),
        cost_estimate=pl.CostEstimate(
            flops=2 * rows * width * EXPERTS * hidden_share,
            bytes_accessed=2 * width * (rows + EXPERTS * hidden_share),
            transcendentals=0,
        ),
    )(upstream, weights)


def expert_line(expert_ref, rows):
    block = lax.broadcasted_iota(jnp.int32, (1, rows), 1) // BLOCK
    line = jnp.zeros((1, rows), jnp.float32)
    for index in range(rows // BLOCK):
        line = jnp.where(block == index, expert_ref[index].astype(jnp.float32), line)
    return line


def column_of(line):
    return jnp.broadcast_to(line, (8, line.shape[1])).T[:, :1]


def factor_of_tokens(gate_pre, up_pre, gate_prob, row_token, block_expert, blk_index, columns):
    rows, hidden_share = gate_pre.shape
    quarter = rows // columns

    def kernel(expert_ref, index_ref, gate_ref, up_ref, prob_ref, token_ref, out_ref):
        gate_value = gate_ref[...].astype(jnp.float32)
        hidden = gate_value * jax.nn.sigmoid(gate_value) * up_ref[...].astype(jnp.float32)
        weighted = (hidden * column_of(prob_ref[...].reshape(1, rows))).astype(jnp.bfloat16)
        place = lax.broadcasted_iota(jnp.int32, (rows, rows), 0)
        part = place // quarter
        token = (index_ref[0] ^ part) * quarter + (place - part * quarter)
        choose = jnp.where(token == token_ref[...].reshape(1, rows), 1.0, 0.0).astype(jnp.bfloat16)
        out_ref[:rows, :] = jnp.dot(choose, weighted, preferred_element_type=jnp.float32)
        experts = jnp.broadcast_to(expert_line(expert_ref, rows), (8, rows)).astype(jnp.bfloat16)
        marks = lax.dot_general(
            experts, choose, (((1,), (1,)), ((), ())), preferred_element_type=jnp.float32
        )
        out_ref[rows:, :] = jnp.zeros((8, hidden_share), jnp.float32)
        for first in range(0, rows, hidden_share):
            amount = min(hidden_share, rows - first)
            line = rows + first // hidden_share
            out_ref[line : line + 1, :amount] = marks[:1, first : first + amount]

    smem, vmem = pl.BlockSpec(memory_space=pltpu.SMEM), pl.BlockSpec(memory_space=pltpu.VMEM)
    return pl.pallas_call(
        kernel,
        out_shape=jax.ShapeDtypeStruct((rows + 8, hidden_share), jnp.float32),
        in_specs=[smem] * 2 + [vmem] * 4,
        out_specs=vmem,
        compiler_params=pltpu.CompilerParams(vmem_limit_bytes=VMEM),
        cost_estimate=pl.CostEstimate(flops=2 * rows * rows * hidden_share, bytes_accessed=12 * rows * hidden_share, transcendentals=0),
    )(block_expert, blk_index.reshape(1), gate_pre, up_pre, gate_prob, row_token)


def row_gradients(both, gate_pre, up_pre, gate_prob, row_token, block_expert):
    rows, hidden_share = gate_pre.shape

    def kernel(expert_ref, both_ref, gate_ref, up_ref, prob_ref, token_ref, up_grad_ref, gate_grad_ref, part_ref):
        place = lax.broadcasted_iota(jnp.int32, (rows, rows), 0)
        mine = place == token_ref[...].reshape(1, rows)
        expert_of_token = jnp.sum(jnp.where(mine, expert_line(expert_ref, rows), 0.0), axis=1, keepdims=True)
        of_token = both_ref[0]
        for expert in range(1, EXPERTS):
            of_token = jnp.where(expert_of_token == float(expert), both_ref[expert], of_token)
        choose = jnp.where(mine, 1.0, 0.0).astype(jnp.bfloat16)
        projected = jnp.zeros((rows, hidden_share), jnp.float32)
        rest = of_token
        for _ in range(3):
            top = rest.astype(jnp.bfloat16)
            projected = projected + lax.dot_general(
                choose, top, (((0,), (0,)), ((), ())), preferred_element_type=jnp.float32
            )
            rest = rest - top.astype(jnp.float32)
        gate_value = gate_ref[...].astype(jnp.float32)
        up_value = up_ref[...].astype(jnp.float32)
        sigmoid_gate = jax.nn.sigmoid(gate_value)
        active = gate_value * sigmoid_gate
        scaled = column_of(prob_ref[...].reshape(1, rows)) * projected
        up_grad_ref[...] = (scaled * active).astype(jnp.bfloat16)
        gate_grad_ref[...] = (
            scaled * up_value * sigmoid_gate * (1.0 + gate_value * (1.0 - sigmoid_gate))
        ).astype(jnp.bfloat16)
        part = jnp.sum(active * up_value * projected, axis=1, keepdims=True)
        part_ref[...] = jnp.broadcast_to(part, (rows, 128)).T[:8, :]

    smem, vmem = pl.BlockSpec(memory_space=pltpu.SMEM), pl.BlockSpec(memory_space=pltpu.VMEM)
    return pl.pallas_call(
        kernel,
        out_shape=[
            jax.ShapeDtypeStruct((rows, hidden_share), jnp.bfloat16),
            jax.ShapeDtypeStruct((rows, hidden_share), jnp.bfloat16),
            jax.ShapeDtypeStruct((8, rows), jnp.float32),
        ],
        in_specs=[smem] + [vmem] * 5,
        out_specs=[vmem] * 3,
        compiler_params=pltpu.CompilerParams(vmem_limit_bytes=16 * 1024 * 1024),
        cost_estimate=pl.CostEstimate(flops=6 * rows * rows * hidden_share, bytes_accessed=20 * rows * hidden_share, transcendentals=0),
    )(block_expert, both, gate_pre, up_pre, gate_prob, row_token)


def together(*values):
    return lax.optimization_barrier(values)


def factors_body(upstream, gate_pre, up_pre, down_weight, block_expert, row_token, gate_prob):
    rows, width = upstream.shape
    hidden_share = gate_pre.shape[1]
    columns = lax.axis_size("blk")
    wide = lax.axis_size("wide")
    chips = wide // 2
    quarter = rows // columns
    half = quarter // 2
    share = width // wide
    blk_index = lax.axis_index("blk")
    wide_index = lax.axis_index("wide")
    chip = wide_index // 2
    core = wide_index % 2

    def moved(value, target):
        pairs = []
        for b in range(columns):
            for z in range(chips):
                for c in range(2):
                    to = target(b, z, c)
                    pairs.append((b * wide + z * 2 + c, to[0] * wide + to[1] * 2 + to[2]))
        return lax.ppermute(value, ("blk", "wide"), pairs)

    def along_x(value):
        return moved(value, lambda b, z, c: (b ^ 1, z, c))

    def along_y(value):
        return moved(value, lambda b, z, c: (b ^ 2, z, c))

    def across(value):
        return moved(value, lambda b, z, c: (b, z, 1 - c))

    def outer_swap(value):
        return moved(value, lambda b, z, c: (b, z ^ 1, c))

    def middle_swap(value):
        return moved(value, lambda b, z, c: (b, 3 - z, c) if 0 < z < 3 else (b, z, 1 - c))

    def piece_for(key, index):
        offset, flip = key
        first_column = share * (2 * (chip ^ offset) + (core ^ flip))
        piece = lax.dynamic_slice(upstream, (quarter * index, first_column), (quarter, share))
        return piece.astype(jnp.float32)

    def sent(key, piece):
        offset, flip = key
        return moved(piece, lambda b, z, c: (b, z ^ offset, c ^ flip))

    near_0 = sent((1, 0), piece_for((1, 0), blk_index))
    skip_0 = sent((2, 0), piece_for((2, 0), blk_index))
    piece_11, piece_21 = piece_for((1, 1), blk_index), piece_for((2, 1), blk_index)
    factor = factor_of_tokens(gate_pre, up_pre, gate_prob, row_token, block_expert, blk_index, columns)
    mid_own = middle_swap(factor)
    other_factor = across(factor)

    def own_columns(of_core, index):
        first_column = share * (2 * chip + of_core)
        parts = [
            lax.dynamic_slice(upstream, (quarter * (index ^ q), first_column), (quarter, share))
            for q in range(columns)
        ]
        return jnp.concatenate(parts, axis=0).astype(jnp.float32)

    down_weight, index, _ = together(down_weight, blk_index, factor)
    weights = jnp.transpose(down_weight, (1, 0, 2))

    token = None

    def arrive(*values, marked=(), flops=0):
        nonlocal token
        if marked:
            token = marker(marked + (() if token is None else (token,)), flops)
        if token is None:
            return together(*values) if len(values) > 1 else values
        *values, token = together(*values, token)
        return values

    half = quarter // 2

    near_0, skip_0, index, weights, piece_11 = arrive(near_0, skip_0, index, weights, piece_11)
    near_1 = sent((1, 1), piece_11)
    (spread,) = stack_rows([[(near_0, 0, quarter), (skip_0, 0, quarter)]], EARLY)
    sent_0 = spread
    x_0, y_0 = along_x(spread), along_y(spread)

    mid_own, factor, piece_21, other_factor, index = arrive(
        mid_own, factor, piece_21, other_factor, index, marked=(mid_own, spread), flops=EARLY
    )
    piece_30, piece_31 = [piece_for(key, index) for key in ((3, 0), (3, 1))]
    own_tokens, other_tokens = own_columns(core, index), own_columns(1 - core, index)
    skip_1 = sent((2, 1), piece_21)

    x_0, y_0, near_1, piece_30, piece_31, other_tokens, own_tokens = arrive(
        x_0, y_0, near_1, piece_30, piece_31, other_tokens, own_tokens
    )
    to_x, to_y = stack_rows(
        [
            [(near_1, 0, quarter), (y_0, quarter, quarter)],
            [(near_1, 0, quarter), (x_0, 0, quarter)],
        ],
        EARLY,
    )
    sent_1 = to_x
    x_1, y_1 = along_x(to_x), along_y(to_y)

    skip_1, piece_30, factor, weights = arrive(
        skip_1, piece_30, factor, weights, marked=(skip_1, to_x), flops=EARLY
    )
    far_0 = sent((3, 0), piece_30)
    both = project(upstream, weights)

    x_1, y_1, other_tokens, both, factor = arrive(x_1, y_1, other_tokens, both, factor)
    factor_near = outer_swap(factor)
    to_x, to_y = stack_rows(
        [
            [(skip_1, 0, quarter), (y_1, half, half)],
            [(skip_1, 0, quarter), (x_1, 0, half)],
        ],
        EARLY,
    )
    sent_2 = to_x
    x_2, y_2 = along_x(to_x), along_y(to_y)
    other_tokens = across(other_tokens)

    far_0, piece_31, mid_own = arrive(far_0, piece_31, mid_own, marked=(far_0, to_x), flops=EARLY)
    far_1 = sent((3, 1), piece_31)
    out_own = outer_swap(mid_own)

    x_2, y_2, factor_near, other_tokens = arrive(x_2, y_2, factor_near, other_tokens)
    to_x, to_y = stack_rows(
        [
            [(far_0, 0, quarter), (y_2, half, half)],
            [(far_0, 0, quarter), (x_2, 0, half)],
        ],
        EARLY,
    )
    sent_3 = to_x
    x_3, y_3 = along_x(to_x), along_y(to_y)
    near_factor = across(factor_near)

    far_1, factor_near, gate_pre = arrive(far_1, factor_near, gate_pre, marked=(far_1, to_x), flops=EARLY)
    mid_near = middle_swap(factor_near)
    up_grad, gate_grad, partial_value = row_gradients(both, gate_pre, up_pre, gate_prob, row_token, block_expert)

    x_3, y_3, near_factor, partial_value, up_grad, gate_grad, own_tokens = arrive(
        x_3, y_3, near_factor, partial_value, up_grad, gate_grad, own_tokens
    )
    to_x, to_y = stack_rows(
        [
            [(far_1, 0, quarter), (y_3, half, half)],
            [(far_1, 0, quarter), (x_3, 0, half)],
        ],
        EARLY,
    )
    sent_4 = to_x
    x_4, y_4 = along_x(to_x), along_y(to_y)
    partial_value = partial_value + along_x(partial_value)

    mid_near, mid_own, out_own = arrive(mid_near, mid_own, out_own, marked=(mid_near, to_x), flops=EARLY)
    out_near = outer_swap(mid_near)
    outer = (chip == 0) | (chip == chips - 1)
    factor_skip = jnp.where(outer, out_own, mid_near)
    skip_factor = across(factor_skip)

    def hopped(own, own_row, x_hop, y_hop, row, diagonal):
        parts = [own, x_hop, y_hop] + [hop for hop, _, _ in diagonal]
        pieces = [(0, own_row, quarter, 0), (1, row, quarter, quarter), (2, row, quarter, 2 * quarter)]
        spot = 3 * quarter
        for index, (_, first, amount) in enumerate(diagonal):
            pieces.append((3 + index, first, amount, spot))
            spot += amount
        return parts, pieces

    def both_sides(one, two):
        shift = len(one[0])
        pieces = one[1] + [(part + shift, first, amount, spot + rows) for part, first, amount, spot in two[1]]
        return tuple(one[0] + two[0]), tuple(pieces)

    total = add_products(
        (own_tokens, other_tokens),
        ((0, 0, rows, 0), (1, 0, rows, rows)),
        (factor, other_factor),
        jnp.zeros((share, EXPERTS * hidden_share), jnp.float32),
        rows,
    )
    total = add_products(
        *both_sides(
            hopped(sent_0, 0, x_0, y_0, 0, ((y_1, quarter, quarter),)),
            hopped(sent_1, 0, x_1, y_1, 0, ((y_2, quarter, half), (x_2, quarter, half))),
        ),
        (factor_near, near_factor), total, rows,
    )
    total = add_products(
        *both_sides(
            hopped(sent_0, quarter, x_0, y_0, quarter, ((x_1, quarter, quarter),)),
            hopped(sent_2, 0, x_2, y_2, 0, ((y_3, quarter, half), (x_3, quarter, half))),
        ),
        (factor_skip, skip_factor), total, rows,
    )

    x_4, y_4, partial_value = arrive(x_4, y_4, partial_value)
    to_x, to_y = stack_rows([[(y_4, half, half)], [(x_4, 0, half)]], LITTLE)
    x_5, y_5 = along_x(to_x), along_y(to_y)
    prob_grad = (partial_value + along_y(partial_value))[0]
    factor_far = jnp.where(outer, out_near, mid_own)
    far_factor = across(factor_far)
    parts, pieces = both_sides(
        hopped(sent_3, 0, x_3, y_3, 0, ((y_4, quarter, half), (x_4, quarter, half))),
        hopped(sent_4, 0, x_4, y_4, 0, ()),
    )
    total = add_products(parts, pieces, (factor_far, far_factor), total, rows)
    x_5, y_5 = arrive(x_5, y_5, marked=(x_5, y_5), flops=EARLY)
    devices = columns * wide
    total, sums = add_products(
        (y_5, x_5),
        ((0, 0, half, 3 * quarter), (1, 0, half, 3 * quarter + half)),
        (far_factor,), total, rows, devices, token,
    )

    down_grad = total.reshape(share, EXPERTS, hidden_share)
    spread = lax.all_to_all(sums, ("blk", "wide"), 0, 0, tiled=True)
    total_sum = jnp.sum(spread, axis=0)[:EXPERTS]
    grad_rms = jnp.sqrt(total_sum / float(D * FFW))
    return (down_grad, grad_rms, prob_grad, gate_grad, up_grad)


def sums_body(upstream, gate_pre, up_pre, down_weight, block_expert, row_token, gate_prob):
    routed = upstream[row_token]
    row_count = routed.shape[0]
    block_count = row_count // BLOCK
    width = routed.shape[1]
    hidden_share = gate_pre.shape[1]
    gate_value = gate_pre.astype(jnp.float32)
    up_value = up_pre.astype(jnp.float32)
    sigmoid_gate = jax.nn.sigmoid(gate_value)
    active = gate_value * sigmoid_gate
    hidden = active * up_value
    weighted = (hidden * gate_prob[:, None]).astype(jnp.bfloat16)
    routed_blocks = routed.reshape(block_count, BLOCK, width)
    weighted_blocks = weighted.reshape(block_count, BLOCK, hidden_share)

    def project(block_item):
        rows_block, expert_id = block_item
        weights = lax.dynamic_index_in_dim(down_weight, expert_id, 1, keepdims=False)
        return jnp.dot(rows_block, weights, preferred_element_type=jnp.float32)

    projected = lax.map(project, (routed_blocks, block_expert)).reshape(row_count, hidden_share)
    scaled = gate_prob[:, None] * projected
    up_grad = (scaled * active).astype(jnp.bfloat16)
    gate_grad = (
        scaled * up_value * sigmoid_gate * (1.0 + gate_value * (1.0 - sigmoid_gate))
    ).astype(jnp.bfloat16)
    partial_value = jnp.sum(hidden * projected, axis=1)
    prob_grad = lax.psum(partial_value, "blk")
    row_share = width // lax.axis_size("wide")

    def select_columns(amount):
        return routed.reshape(block_count, BLOCK, amount)

    def block_product(columns, block_index):
        column_block = lax.dynamic_index_in_dim(columns, block_index, 0, keepdims=False)
        weighted_block = lax.dynamic_index_in_dim(weighted_blocks, block_index, 0, keepdims=False)
        return jnp.dot(column_block.T, weighted_block, preferred_element_type=jnp.float32)

    pieces = []
    for expert in range(EXPERTS):

        def one_expert(first, amount, expert=expert):
            columns = select_columns(amount)

            def add_block(block_index, running):
                expert_id = lax.dynamic_index_in_dim(block_expert, block_index, 0, keepdims=False)

                def with_block(running_sum):
                    return running_sum + block_product(columns, block_index)

                def without_block(running_sum):
                    return running_sum

                return lax.cond(expert_id == expert, with_block, without_block, running)

            start_value = jnp.zeros((amount, hidden_share), jnp.float32)
            return lax.fori_loop(0, block_count, add_block, start_value)

        pieces.append(
            lax.psum_scatter(
                one_expert(jnp.int32(0), lax.axis_size("wide") * row_share),
                "wide",
                scatter_dimension=0,
                tiled=True,
            )
        )
    down_grad = jnp.stack(pieces, axis=1)
    squares = jnp.sum(down_grad * down_grad, axis=(0, 2))
    total_sum = lax.psum(squares, ("blk", "wide"))
    grad_rms = jnp.sqrt(total_sum / float(D * FFW))
    return (down_grad, grad_rms, prob_grad, gate_grad, up_grad)


def solution(mesh):
    columns, wide = mesh.shape["blk"], mesh.shape["wide"]

    def body(upstream, gate_pre, up_pre, down_weight, block_expert, row_token, gate_prob):
        rows, width = upstream.shape
        hidden_share = gate_pre.shape[1]
        factors = wide * rows * (hidden_share + width // wide)
        sums = EXPERTS * width * hidden_share
        plan = factors_body if columns == 4 and wide == 8 and factors < sums else sums_body
        return plan(upstream, gate_pre, up_pre, down_weight, block_expert, row_token, gate_prob)

    in_specs = (
        P("wide", None),
        P("wide", "blk"),
        P("wide", "blk"),
        P(None, None, "blk"),
        P("wide"),
        P("wide"),
        P("wide"),
    )
    out_specs = (P("wide", None, "blk"), P(), P("wide"), P("wide", "blk"), P("wide", "blk"))
    return jax.shard_map(body, mesh=mesh, in_specs=in_specs, out_specs=out_specs, check_vma=False)
```

```python
import jax
import jax.numpy as jnp
from jax import lax
from jax.experimental import pallas as pl
from jax.experimental.pallas import tpu as pltpu
from jax.sharding import PartitionSpec as P

D = 7168
FFW = 1024
EXPERTS = 2
BLOCK = 128
VMEM = 56 * 1024 * 1024
EARLY = 20_000_000_000
LITTLE = 1_000_000_000
STACK_VMEM = 1024 * 1024


def add_products(parts, pieces, factors, total, rows, devices=0, token=None):
    share = parts[0].shape[-1]
    hidden_share = factors[0].shape[1]
    low = pieces[0][3]
    high = pieces[-1][3] + pieces[-1][2]
    last = () if token is None else (token,)
    n_parts, n_factors = len(parts), len(factors)

    def kernel(*refs):
        part_refs, factor_refs = refs[:n_parts], refs[n_parts : n_parts + n_factors]
        total_ref, out_ref = refs[n_parts + n_factors], refs[n_parts + n_factors + 1 + len(last)]
        left, right = refs[-2:]
        for part, first, amount, spot in pieces:
            left[spot - low : spot - low + amount, :] = part_refs[part][first : first + amount, :].astype(jnp.bfloat16)
        for side, factor_ref in enumerate(factor_refs):
            marks = factor_ref[rows:, :].T
            for first in range(0, rows, hidden_share):
                amount = min(hidden_share, rows - first)
                line = first // hidden_share
                begin = max(first, low - side * rows)
                end = min(first + amount, high - side * rows)
                if begin >= end:
                    continue
                mark = marks[begin - first : end - first, line : line + 1]
                weight = factor_ref[begin:end, :]
                spot = side * rows + begin - low
                for expert in range(EXPERTS):
                    right[spot : spot + end - begin, expert * hidden_share : (expert + 1) * hidden_share] = jnp.where(
                        mark == float(expert), weight, 0.0
                    ).astype(jnp.bfloat16)
        weights = right[...]
        squares = jnp.zeros((1, EXPERTS * hidden_share), jnp.float32)
        for first in range(0, share, 128):
            block = total_ref[first : first + 128, :] + lax.dot_general(
                left[:, first : first + 128],
                weights,
                (((0,), (0,)), ((), ())),
                preferred_element_type=jnp.float32,
            )
            out_ref[first : first + 128, :] = block
            if devices:
                squares = squares + jnp.sum(block * block, axis=0, keepdims=True)
        if devices:
            lane = lax.broadcasted_iota(jnp.int32, (devices, 128), 1)
            sums = jnp.zeros((devices, 128), jnp.float32)
            for expert in range(EXPERTS):
                own = squares[:, expert * hidden_share : (expert + 1) * hidden_share]
                sums = jnp.where(lane == expert, jnp.sum(own, axis=1, keepdims=True), sums)
            refs[-3][...] = sums

    depth = high - low
    out_shape = [jax.ShapeDtypeStruct(total.shape, jnp.float32)]
    if devices:
        out_shape.append(jax.ShapeDtypeStruct((devices, 128), jnp.float32))
    results = pl.pallas_call(
        kernel,
        out_shape=out_shape,
        in_specs=[pl.BlockSpec(memory_space=pltpu.VMEM)] * (n_parts + n_factors + 1)
        + [pl.BlockSpec(memory_space=pl.ANY)] * len(last),
        out_specs=[pl.BlockSpec(memory_space=pltpu.VMEM)] * len(out_shape),
        scratch_shapes=[
            pltpu.VMEM((depth, share), jnp.bfloat16),
            pltpu.VMEM((depth, EXPERTS * hidden_share), jnp.bfloat16),
        ],
        compiler_params=pltpu.CompilerParams(vmem_limit_bytes=16 * 1024 * 1024),
        cost_estimate=pl.CostEstimate(
            flops=2 * depth * share * EXPERTS * hidden_share,
            bytes_accessed=4 * depth * (share + hidden_share) + 8 * share * EXPERTS * hidden_share,
            transcendentals=0,
        ),
    )(*parts, *factors, total, *last)
    return results if devices else results[0]


def stack_rows(lists, flops=0):
    arrays = []
    for pieces in lists:
        for array, _, _ in pieces:
            if not any(array is one for one in arrays):
                arrays.append(array)
    places = [
        [([array is one for one in arrays].index(True), first, amount) for array, first, amount in pieces]
        for pieces in lists
    ]
    share = arrays[0].shape[1]
    heights = [sum(amount for _, _, amount in pieces) for pieces in lists]

    def kernel(*refs):
        for out_ref, pieces in zip(refs[len(arrays) :], places):
            spot = 0
            for index, first, amount in pieces:
                out_ref[spot : spot + amount, :] = refs[index][first : first + amount, :]
                spot += amount

    return pl.pallas_call(
        kernel,
        out_shape=[jax.ShapeDtypeStruct((height, share), jnp.float32) for height in heights],
        in_specs=[pl.BlockSpec(memory_space=pltpu.VMEM)] * len(arrays),
        out_specs=[pl.BlockSpec(memory_space=pltpu.VMEM)] * len(lists),
        compiler_params=pltpu.CompilerParams(vmem_limit_bytes=12 * 1024 * 1024),
        cost_estimate=pl.CostEstimate(flops=flops, bytes_accessed=8 * sum(heights) * share, transcendentals=0),
    )(*arrays)


def marker(values, flops):
    def kernel(*refs):
        refs[-1][...] = jnp.zeros_like(refs[-1])

    return pl.pallas_call(
        kernel,
        out_shape=jax.ShapeDtypeStruct((8, 128), jnp.float32),
        in_specs=[pl.BlockSpec(memory_space=pl.ANY)] * len(values),
        out_specs=pl.BlockSpec(memory_space=pltpu.VMEM),
        compiler_params=pltpu.CompilerParams(vmem_limit_bytes=1024 * 1024),
        cost_estimate=pl.CostEstimate(flops=flops, bytes_accessed=8192, transcendentals=0),
    )(*values)


def project(upstream, weights):
    rows, width = upstream.shape
    hidden_share = weights.shape[2]
    steps = 4 if width % (4 * 128) == 0 else 1
    block = width // steps

    def kernel(upstream_ref, weights_ref, out_ref):
        @pl.when(pl.program_id(0) == 0)
        def _():
            out_ref[...] = jnp.zeros_like(out_ref)

        for expert in range(EXPERTS):
            out_ref[expert] += jnp.dot(
                upstream_ref[...], weights_ref[expert], preferred_element_type=jnp.float32
            )

    return pl.pallas_call(
        kernel,
        out_shape=jax.ShapeDtypeStruct((EXPERTS, rows, hidden_share), jnp.float32),
        grid=(steps,),
        in_specs=[
            pl.BlockSpec((rows, block), lambda i: (0, i)),
            pl.BlockSpec((EXPERTS, block, hidden_share), lambda i: (0, i, 0)),
        ],
        out_specs=pl.BlockSpec((EXPERTS, rows, hidden_share), lambda i: (0, 0, 0)),
        compiler_params=pltpu.CompilerParams(vmem_limit_bytes=16 * 1024 * 1024),
        cost_estimate=pl.CostEstimate(
            flops=2 * rows * width * EXPERTS * hidden_share,
            bytes_accessed=2 * width * (rows + EXPERTS * hidden_share),
            transcendentals=0,
        ),
    )(upstream, weights)


def expert_line(expert_ref, rows):
    block = lax.broadcasted_iota(jnp.int32, (1, rows), 1) // BLOCK
    line = jnp.zeros((1, rows), jnp.float32)
    for index in range(rows // BLOCK):
        line = jnp.where(block == index, expert_ref[index].astype(jnp.float32), line)
    return line


def column_of(line):
    return jnp.broadcast_to(line, (8, line.shape[1])).T[:, :1]


def factor_of_tokens(gate_pre, up_pre, gate_prob, row_token, block_expert, blk_index, columns):
    rows, hidden_share = gate_pre.shape
    quarter = rows // columns

    def kernel(expert_ref, index_ref, gate_ref, up_ref, prob_ref, token_ref, out_ref):
        gate_value = gate_ref[...].astype(jnp.float32)
        hidden = gate_value * jax.nn.sigmoid(gate_value) * up_ref[...].astype(jnp.float32)
        weighted = (hidden * column_of(prob_ref[...].reshape(1, rows))).astype(jnp.bfloat16)
        place = lax.broadcasted_iota(jnp.int32, (rows, rows), 0)
        part = place // quarter
        token = (index_ref[0] ^ part) * quarter + (place - part * quarter)
        choose = jnp.where(token == token_ref[...].reshape(1, rows), 1.0, 0.0).astype(jnp.bfloat16)
        out_ref[:rows, :] = jnp.dot(choose, weighted, preferred_element_type=jnp.float32)
        experts = jnp.broadcast_to(expert_line(expert_ref, rows), (8, rows)).astype(jnp.bfloat16)
        marks = lax.dot_general(
            experts, choose, (((1,), (1,)), ((), ())), preferred_element_type=jnp.float32
        )
        out_ref[rows:, :] = jnp.zeros((8, hidden_share), jnp.float32)
        for first in range(0, rows, hidden_share):
            amount = min(hidden_share, rows - first)
            line = rows + first // hidden_share
            out_ref[line : line + 1, :amount] = marks[:1, first : first + amount]

    smem, vmem = pl.BlockSpec(memory_space=pltpu.SMEM), pl.BlockSpec(memory_space=pltpu.VMEM)
    return pl.pallas_call(
        kernel,
        out_shape=jax.ShapeDtypeStruct((rows + 8, hidden_share), jnp.float32),
        in_specs=[smem] * 2 + [vmem] * 4,
        out_specs=vmem,
        compiler_params=pltpu.CompilerParams(vmem_limit_bytes=VMEM),
        cost_estimate=pl.CostEstimate(flops=2 * rows * rows * hidden_share, bytes_accessed=12 * rows * hidden_share, transcendentals=0),
    )(block_expert, blk_index.reshape(1), gate_pre, up_pre, gate_prob, row_token)


def row_gradients(both, gate_pre, up_pre, gate_prob, row_token, block_expert):
    rows, hidden_share = gate_pre.shape

    def kernel(expert_ref, both_ref, gate_ref, up_ref, prob_ref, token_ref, up_grad_ref, gate_grad_ref, part_ref):
        place = lax.broadcasted_iota(jnp.int32, (rows, rows), 0)
        mine = place == token_ref[...].reshape(1, rows)
        expert_of_token = jnp.sum(jnp.where(mine, expert_line(expert_ref, rows), 0.0), axis=1, keepdims=True)
        of_token = both_ref[0]
        for expert in range(1, EXPERTS):
            of_token = jnp.where(expert_of_token == float(expert), both_ref[expert], of_token)
        choose = jnp.where(mine, 1.0, 0.0).astype(jnp.bfloat16)
        projected = jnp.zeros((rows, hidden_share), jnp.float32)
        rest = of_token
        for _ in range(3):
            top = rest.astype(jnp.bfloat16)
            projected = projected + lax.dot_general(
                choose, top, (((0,), (0,)), ((), ())), preferred_element_type=jnp.float32
            )
            rest = rest - top.astype(jnp.float32)
        gate_value = gate_ref[...].astype(jnp.float32)
        up_value = up_ref[...].astype(jnp.float32)
        sigmoid_gate = jax.nn.sigmoid(gate_value)
        active = gate_value * sigmoid_gate
        scaled = column_of(prob_ref[...].reshape(1, rows)) * projected
        up_grad_ref[...] = (scaled * active).astype(jnp.bfloat16)
        gate_grad_ref[...] = (
            scaled * up_value * sigmoid_gate * (1.0 + gate_value * (1.0 - sigmoid_gate))
        ).astype(jnp.bfloat16)
        part = jnp.sum(active * up_value * projected, axis=1, keepdims=True)
        part_ref[...] = jnp.broadcast_to(part, (rows, 128)).T[:8, :]

    smem, vmem = pl.BlockSpec(memory_space=pltpu.SMEM), pl.BlockSpec(memory_space=pltpu.VMEM)
    return pl.pallas_call(
        kernel,
        out_shape=[
            jax.ShapeDtypeStruct((rows, hidden_share), jnp.bfloat16),
            jax.ShapeDtypeStruct((rows, hidden_share), jnp.bfloat16),
            jax.ShapeDtypeStruct((8, rows), jnp.float32),
        ],
        in_specs=[smem] + [vmem] * 5,
        out_specs=[vmem] * 3,
        compiler_params=pltpu.CompilerParams(vmem_limit_bytes=16 * 1024 * 1024),
        cost_estimate=pl.CostEstimate(flops=6 * rows * rows * hidden_share, bytes_accessed=20 * rows * hidden_share, transcendentals=0),
    )(block_expert, both, gate_pre, up_pre, gate_prob, row_token)


def together(*values):
    return lax.optimization_barrier(values)


def factors_body(upstream, gate_pre, up_pre, down_weight, block_expert, row_token, gate_prob):
    rows, width = upstream.shape
    hidden_share = gate_pre.shape[1]
    columns = lax.axis_size("blk")
    wide = lax.axis_size("wide")
    chips = wide // 2
    quarter = rows // columns
    half = quarter // 2
    share = width // wide
    blk_index = lax.axis_index("blk")
    wide_index = lax.axis_index("wide")
    chip = wide_index // 2
    core = wide_index % 2

    def moved(value, target):
        pairs = []
        for b in range(columns):
            for z in range(chips):
                for c in range(2):
                    to = target(b, z, c)
                    pairs.append((b * wide + z * 2 + c, to[0] * wide + to[1] * 2 + to[2]))
        return lax.ppermute(value, ("blk", "wide"), pairs)

    def along_x(value):
        return moved(value, lambda b, z, c: (b ^ 1, z, c))

    def along_y(value):
        return moved(value, lambda b, z, c: (b ^ 2, z, c))

    def across(value):
        return moved(value, lambda b, z, c: (b, z, 1 - c))

    def outer_swap(value):
        return moved(value, lambda b, z, c: (b, z ^ 1, c))

    def middle_swap(value):
        return moved(value, lambda b, z, c: (b, 3 - z, c) if 0 < z < 3 else (b, z, 1 - c))

    def piece_for(key, index):
        offset, flip = key
        first_column = share * (2 * (chip ^ offset) + (core ^ flip))
        piece = lax.dynamic_slice(upstream, (quarter * index, first_column), (quarter, share))
        return piece.astype(jnp.float32)

    def sent(key, piece):
        offset, flip = key
        return moved(piece, lambda b, z, c: (b, z ^ offset, c ^ flip))

    near_0 = sent((1, 0), piece_for((1, 0), blk_index))
    skip_0 = sent((2, 0), piece_for((2, 0), blk_index))
    piece_11, piece_21 = piece_for((1, 1), blk_index), piece_for((2, 1), blk_index)
    factor = factor_of_tokens(gate_pre, up_pre, gate_prob, row_token, block_expert, blk_index, columns)
    mid_own = middle_swap(factor)
    other_factor = across(factor)

    def own_columns(of_core, index):
        first_column = share * (2 * chip + of_core)
        parts = [
            lax.dynamic_slice(upstream, (quarter * (index ^ q), first_column), (quarter, share))
            for q in range(columns)
        ]
        return jnp.concatenate(parts, axis=0).astype(jnp.float32)

    down_weight, index, _ = together(down_weight, blk_index, factor)
    weights = jnp.transpose(down_weight, (1, 0, 2))

    token = None

    def arrive(*values, marked=(), flops=0):
        nonlocal token
        if marked:
            token = marker(marked + (() if token is None else (token,)), flops)
        if token is None:
            return together(*values) if len(values) > 1 else values
        *values, token = together(*values, token)
        return values

    half = quarter // 2

    near_0, skip_0, index, weights, piece_11 = arrive(near_0, skip_0, index, weights, piece_11)
    near_1 = sent((1, 1), piece_11)
    (spread,) = stack_rows([[(near_0, 0, quarter), (skip_0, 0, quarter)]], EARLY)
    sent_0 = spread
    x_0, y_0 = along_x(spread), along_y(spread)

    mid_own, factor, piece_21, other_factor, index = arrive(
        mid_own, factor, piece_21, other_factor, index, marked=(mid_own, spread), flops=EARLY
    )
    piece_30, piece_31 = [piece_for(key, index) for key in ((3, 0), (3, 1))]
    own_tokens, other_tokens = own_columns(core, index), own_columns(1 - core, index)
    skip_1 = sent((2, 1), piece_21)

    x_0, y_0, near_1, piece_30, piece_31, other_tokens, own_tokens = arrive(
        x_0, y_0, near_1, piece_30, piece_31, other_tokens, own_tokens
    )
    to_x, to_y = stack_rows(
        [
            [(near_1, 0, quarter), (y_0, quarter, quarter)],
            [(near_1, 0, quarter), (x_0, 0, quarter)],
        ],
        EARLY,
    )
    sent_1 = to_x
    x_1, y_1 = along_x(to_x), along_y(to_y)

    skip_1, piece_30, factor, weights = arrive(
        skip_1, piece_30, factor, weights, marked=(skip_1, to_x), flops=EARLY
    )
    far_0 = sent((3, 0), piece_30)
    both = project(upstream, weights)

    x_1, y_1, other_tokens, both, factor = arrive(x_1, y_1, other_tokens, both, factor)
    factor_near = outer_swap(factor)
    to_x, to_y = stack_rows(
        [
            [(skip_1, 0, quarter), (y_1, half, half)],
            [(skip_1, 0, quarter), (x_1, 0, half)],
        ],
        EARLY,
    )
    sent_2 = to_x
    x_2, y_2 = along_x(to_x), along_y(to_y)
    other_tokens = across(other_tokens)

    far_0, piece_31, mid_own = arrive(far_0, piece_31, mid_own, marked=(far_0, to_x), flops=EARLY)
    far_1 = sent((3, 1), piece_31)
    out_own = outer_swap(mid_own)

    x_2, y_2, factor_near, other_tokens = arrive(x_2, y_2, factor_near, other_tokens)
    to_x, to_y = stack_rows(
        [
            [(far_0, 0, quarter), (y_2, half, half)],
            [(far_0, 0, quarter), (x_2, 0, half)],
        ],
        EARLY,
    )
    sent_3 = to_x
    x_3, y_3 = along_x(to_x), along_y(to_y)
    near_factor = across(factor_near)

    far_1, factor_near, gate_pre = arrive(far_1, factor_near, gate_pre, marked=(far_1, to_x), flops=EARLY)
    mid_near = middle_swap(factor_near)
    up_grad, gate_grad, partial_value = row_gradients(both, gate_pre, up_pre, gate_prob, row_token, block_expert)

    x_3, y_3, near_factor, partial_value, up_grad, gate_grad, own_tokens = arrive(
        x_3, y_3, near_factor, partial_value, up_grad, gate_grad, own_tokens
    )
    to_x, to_y = stack_rows(
        [
            [(far_1, 0, quarter), (y_3, half, half)],
            [(far_1, 0, quarter), (x_3, 0, half)],
        ],
        EARLY,
    )
    sent_4 = to_x
    x_4, y_4 = along_x(to_x), along_y(to_y)

    mid_near, mid_own, out_own, partial_value = arrive(
        mid_near, mid_own, out_own, partial_value, marked=(mid_near, to_x), flops=EARLY
    )
    partial_value = partial_value + along_x(partial_value)
    out_near = outer_swap(mid_near)
    outer = (chip == 0) | (chip == chips - 1)
    factor_skip = jnp.where(outer, out_own, mid_near)
    skip_factor = across(factor_skip)

    def hopped(own, own_row, x_hop, y_hop, row, diagonal):
        parts = [own, x_hop, y_hop] + [hop for hop, _, _ in diagonal]
        pieces = [(0, own_row, quarter, 0), (1, row, quarter, quarter), (2, row, quarter, 2 * quarter)]
        spot = 3 * quarter
        for index, (_, first, amount) in enumerate(diagonal):
            pieces.append((3 + index, first, amount, spot))
            spot += amount
        return parts, pieces

    def both_sides(one, two):
        shift = len(one[0])
        pieces = one[1] + [(part + shift, first, amount, spot + rows) for part, first, amount, spot in two[1]]
        return tuple(one[0] + two[0]), tuple(pieces)

    total = add_products(
        (own_tokens, other_tokens),
        ((0, 0, rows, 0), (1, 0, rows, rows)),
        (factor, other_factor),
        jnp.zeros((share, EXPERTS * hidden_share), jnp.float32),
        rows,
    )
    total = add_products(
        *both_sides(
            hopped(sent_0, 0, x_0, y_0, 0, ((y_1, quarter, quarter),)),
            hopped(sent_1, 0, x_1, y_1, 0, ((y_2, quarter, half), (x_2, quarter, half))),
        ),
        (factor_near, near_factor), total, rows,
    )
    total = add_products(
        *both_sides(
            hopped(sent_0, quarter, x_0, y_0, quarter, ((x_1, quarter, quarter),)),
            hopped(sent_2, 0, x_2, y_2, 0, ((y_3, quarter, half), (x_3, quarter, half))),
        ),
        (factor_skip, skip_factor), total, rows,
    )

    x_4, y_4, partial_value = arrive(x_4, y_4, partial_value)
    to_x, to_y = stack_rows([[(y_4, half, half)], [(x_4, 0, half)]], LITTLE)
    x_5, y_5 = along_x(to_x), along_y(to_y)
    prob_grad = (partial_value + along_y(partial_value))[0]
    factor_far = jnp.where(outer, out_near, mid_own)
    far_factor = across(factor_far)
    parts, pieces = both_sides(
        hopped(sent_3, 0, x_3, y_3, 0, ((y_4, quarter, half), (x_4, quarter, half))),
        hopped(sent_4, 0, x_4, y_4, 0, ()),
    )
    total = add_products(parts, pieces, (factor_far, far_factor), total, rows)
    x_5, y_5 = arrive(x_5, y_5, marked=(x_5, y_5), flops=EARLY)
    devices = columns * wide
    total, sums = add_products(
        (y_5, x_5),
        ((0, 0, half, 3 * quarter), (1, 0, half, 3 * quarter + half)),
        (far_factor,), total, rows, devices, token,
    )

    down_grad = total.reshape(share, EXPERTS, hidden_share)
    spread = lax.all_to_all(sums, ("blk", "wide"), 0, 0, tiled=True)
    total_sum = jnp.sum(spread, axis=0)[:EXPERTS]
    grad_rms = jnp.sqrt(total_sum / float(D * FFW))
    return (down_grad, grad_rms, prob_grad, gate_grad, up_grad)


def sums_body(upstream, gate_pre, up_pre, down_weight, block_expert, row_token, gate_prob):
    routed = upstream[row_token]
    row_count = routed.shape[0]
    block_count = row_count // BLOCK
    width = routed.shape[1]
    hidden_share = gate_pre.shape[1]
    gate_value = gate_pre.astype(jnp.float32)
    up_value = up_pre.astype(jnp.float32)
    sigmoid_gate = jax.nn.sigmoid(gate_value)
    active = gate_value * sigmoid_gate
    hidden = active * up_value
    weighted = (hidden * gate_prob[:, None]).astype(jnp.bfloat16)
    routed_blocks = routed.reshape(block_count, BLOCK, width)
    weighted_blocks = weighted.reshape(block_count, BLOCK, hidden_share)

    def project(block_item):
        rows_block, expert_id = block_item
        weights = lax.dynamic_index_in_dim(down_weight, expert_id, 1, keepdims=False)
        return jnp.dot(rows_block, weights, preferred_element_type=jnp.float32)

    projected = lax.map(project, (routed_blocks, block_expert)).reshape(row_count, hidden_share)
    scaled = gate_prob[:, None] * projected
    up_grad = (scaled * active).astype(jnp.bfloat16)
    gate_grad = (
        scaled * up_value * sigmoid_gate * (1.0 + gate_value * (1.0 - sigmoid_gate))
    ).astype(jnp.bfloat16)
    partial_value = jnp.sum(hidden * projected, axis=1)
    prob_grad = lax.psum(partial_value, "blk")
    row_share = width // lax.axis_size("wide")

    def select_columns(amount):
        return routed.reshape(block_count, BLOCK, amount)

    def block_product(columns, block_index):
        column_block = lax.dynamic_index_in_dim(columns, block_index, 0, keepdims=False)
        weighted_block = lax.dynamic_index_in_dim(weighted_blocks, block_index, 0, keepdims=False)
        return jnp.dot(column_block.T, weighted_block, preferred_element_type=jnp.float32)

    pieces = []
    for expert in range(EXPERTS):

        def one_expert(first, amount, expert=expert):
            columns = select_columns(amount)

            def add_block(block_index, running):
                expert_id = lax.dynamic_index_in_dim(block_expert, block_index, 0, keepdims=False)

                def with_block(running_sum):
                    return running_sum + block_product(columns, block_index)

                def without_block(running_sum):
                    return running_sum

                return lax.cond(expert_id == expert, with_block, without_block, running)

            start_value = jnp.zeros((amount, hidden_share), jnp.float32)
            return lax.fori_loop(0, block_count, add_block, start_value)

        pieces.append(
            lax.psum_scatter(
                one_expert(jnp.int32(0), lax.axis_size("wide") * row_share),
                "wide",
                scatter_dimension=0,
                tiled=True,
            )
        )
    down_grad = jnp.stack(pieces, axis=1)
    squares = jnp.sum(down_grad * down_grad, axis=(0, 2))
    total_sum = lax.psum(squares, ("blk", "wide"))
    grad_rms = jnp.sqrt(total_sum / float(D * FFW))
    return (down_grad, grad_rms, prob_grad, gate_grad, up_grad)


def solution(mesh):
    columns, wide = mesh.shape["blk"], mesh.shape["wide"]

    def body(upstream, gate_pre, up_pre, down_weight, block_expert, row_token, gate_prob):
        rows, width = upstream.shape
        hidden_share = gate_pre.shape[1]
        factors = wide * rows * (hidden_share + width // wide)
        sums = EXPERTS * width * hidden_share
        plan = factors_body if columns == 4 and wide == 8 and factors < sums else sums_body
        return plan(upstream, gate_pre, up_pre, down_weight, block_expert, row_token, gate_prob)

    in_specs = (
        P("wide", None),
        P("wide", "blk"),
        P("wide", "blk"),
        P(None, None, "blk"),
        P("wide"),
        P("wide"),
        P("wide"),
    )
    out_specs = (P("wide", None, "blk"), P(), P("wide"), P("wide", "blk"), P("wide", "blk"))
    return jax.shard_map(body, mesh=mesh, in_specs=in_specs, out_specs=out_specs, check_vma=False)
```
